32 devices in a mesh: dp: 8 (over z, x), replica: 4 (over y, core).
Axes of the slice: x: 2, y: 2, z: 4, core: 2. Of those that a mesh axis runs over, the one named last changes fastest.
Arguments:
- grad_parts: bfloat16 [64, 1024, 512], P('dp', 'replica'), may hold values from -1.1953125 to 1.1953125
- master_weight: float32 [8192, 512], P(('dp', 'replica')), may hold values from -0.0625 to 0.0625
- moment_one: float32 [8192, 512], P(('dp', 'replica')), may hold values from -1.8 to 1.8
- moment_two: float32 [8192, 512], P(('dp', 'replica')), may hold values from 0.05 to 2
- queries: bfloat16 [4, 1024, 4096], P('replica', 'dp'), may hold values from -5 to 5
- keys_in: bfloat16 [4, 1024, 512], P('replica', 'dp'), may hold values from -5 to 5
- hidden: bfloat16 [4, 1024, 8192], P('replica', 'dp'), may hold values from -6 to 6
- segment_ids: int32 [4, 1024], P('replica', 'dp'), may hold values from 0 to 4, never falling along the last dimension, each value on 1 to 384 neighbouring positions
- packed_len: int32 [4], P('replica'), may hold values from 512 to 1024
Outputs:
- new_master: float32 [8192, 512], P(('dp', 'replica'))
- new_first: float32 [8192, 512], P(('dp', 'replica'))
- new_second: float32 [8192, 512], P(('dp', 'replica'))
- attended: bfloat16 [4, 1024, 4096], P('replica', 'dp')
The draws below stay inside these ranges and needn't reach their ends.
Inputs may be any that keep to these rules, and one draw needn't show every extreme that they name: `segment_ids`: on each replica the numbers never fall along positions, and each prompt covers at most 384 positions, one exactly that many.
All inputs are finite; a program needn't handle non-finite values.
Results may differ from the reference program's by a relative error of at most 0.009.
Values may be sent and summed in bfloat16 or wider, within the bound.
No kernel may reach another device: no remote copies, remote signals or barrier semaphores. Data moves between devices by JAX's collectives and lax.ppermute only.
A program may use at most 64 MiB of HBM per device.

```python
import math
import jax
import jax.numpy as jnp
import numpy as np
from jax import lax

D = 8192
HD = 128
KVH = 4
QH = 32
TOK_DEV = 128
C = 512
TOKR = 1024
N_DP = 8
N_REPLICA = 4


def draw_queries(key, part):
    full_shape = (N_REPLICA, TOKR, QH * HD)
    drawn_values = jnp.clip(jax.random.normal(jax.random.fold_in(key, 1), full_shape, jnp.float32), -5.0, 5.0)
    return drawn_values.astype(jnp.bfloat16)


def draw_keys_in(key, part):
    full_shape = (N_REPLICA, TOKR, KVH * HD)
    drawn_values = jnp.clip(jax.random.normal(jax.random.fold_in(key, 2), full_shape, jnp.float32), -5.0, 5.0)
    return drawn_values.astype(jnp.bfloat16)


def set_ends(drawn, own_key, low, largest):
    longest = drawn.shape.index(max(drawn.shape))
    spots = []
    for shift in (0, 1):
        where = [jax.random.randint(jax.random.fold_in(own_key, axis), (), 0, length) for axis, length in enumerate(drawn.shape)]
        where[longest] = (where[longest] + shift) % drawn.shape[longest]
        spots.append(tuple(where))
    return drawn.at[spots[0]].set(low).at[spots[1]].set(largest)


def level_of(stream_key, extent, shards, low, top_value):
    def one(dim, shards_of):
        draws = jax.random.uniform(jax.random.fold_in(jax.random.fold_in(stream_key, 6), dim), (shards_of,), jnp.float32, low / len(shards), top_value / len(shards))
        return jnp.repeat(jnp.exp(draws), extent[dim] // shards_of).reshape((-1,) + (1,) * (len(extent) - dim - 1))

    factor_of = one(*shards[0])
    for cut in shards[1:]:
        factor_of = factor_of * one(*cut)
    return factor_of


def split_up(number_of, total, most, lean):
    portions = [(1 << 20) // math.isqrt(rank ** lean) + 1 for rank in range(2, number_of + 1)]
    spare, holding = total - most - (number_of - 1), [1] * (number_of - 1)
    while spare > 0:
        candidates = [i for i in range(number_of - 1) if holding[i] < most]
        pool, left = sum([portions[i] for i in candidates]), spare
        for i in candidates:
            addition = min(most - holding[i], max(1, left * portions[i] // pool), spare)
            holding[i] = holding[i] + addition
            spare = spare - addition
    return np.array([most] + holding)


def uneven(rng, count, total, limit, skew):
    if count == 2:
        one = jax.random.randint(rng, (), max(1, total - limit), min(limit, total - 1) + 1)
        return jnp.stack([one, total - one])
    tallies = jnp.asarray(split_up(count, total, limit, skew), jnp.int32)
    pairs = (count - 1) // 2
    source_of, receiver = tallies[1:1 + 2 * pairs:2], tallies[2:2 + 2 * pairs:2]
    room = jnp.minimum(source_of - 1, limit - receiver)
    passed = jax.random.randint(jax.random.fold_in(rng, 1), (pairs,), 0, 1 << 20) % (room + 1)
    tallies = tallies.at[1:1 + 2 * pairs:2].set(source_of - passed).at[2:2 + 2 * pairs:2].set(receiver + passed)
    return tallies[jax.random.permutation(jax.random.fold_in(rng, 2), count)]


def normal_values(own_key, dims, spread, limit, shards=(), kind=jnp.bfloat16):
    entries = spread * jax.random.normal(own_key, dims, jnp.float32)
    if shards:
        entries = entries * level_of(own_key, dims, shards, -0.22, 0.18)
    return jnp.clip(entries, -limit, limit).astype(kind)


def setup_inputs(seed: int = 0) -> dict:
    key_of = jax.random.split(jax.random.key(seed), 10)
    grad_parts = normal_values(key_of[0], (N_DP * N_DP, D // N_DP, C), 0.2, 1.1953125, ((0, 8), (1, 4)))
    master_weight = normal_values(key_of[1], (D, C), D ** -0.5, 0.0625, ((0, 32),), jnp.float32)
    moment_one = normal_values(key_of[2], (D, C), 0.3, 1.8, ((0, 32),), jnp.float32)
    moment_two = jnp.clip(jnp.exp(math.log(2.0) - 3.6888794 * jax.random.uniform(key_of[3], (D, C), jnp.float32) ** level_of(key_of[3], (D, C), ((0, 32),), -0.2, 0.2)), 0.05, 2.0)
    queries = draw_queries(jax.random.fold_in(key_of[9], 71), 0)
    keys_in = draw_keys_in(jax.random.fold_in(key_of[9], 71), 0)
    hidden = normal_values(key_of[6], (N_REPLICA, TOKR, D), 1.0, 6.0, ((0, 4), (1, 8)))
    segment_ids = jax.vmap(lambda own: jnp.searchsorted(jnp.cumsum(uneven(own, 2 * N_DP // 3, TOKR, 3 * TOK_DEV, 1)), jnp.arange(TOKR), side="right"))(jax.random.split(key_of[7], N_REPLICA)).reshape((N_REPLICA, TOKR)).astype(jnp.int32)
    packed_len = set_ends(jax.random.randint(key_of[8], (N_REPLICA,), TOKR // 2, TOKR + 1), jax.random.fold_in(key_of[8], 1), TOKR // 2, TOKR).astype(jnp.int32)
    return dict(grad_parts=grad_parts, master_weight=master_weight, moment_one=moment_one, moment_two=moment_two, queries=queries, keys_in=keys_in, hidden=hidden, segment_ids=segment_ids, packed_len=packed_len)


beta_one = 0.9
beta_two = 0.95
bias_one = 1.0 - 0.9 ** 10
bias_two = 1.0 - 0.95 ** 10
adam_eps = 1e-08
learn_rate = 0.002
weight_decay = 0.1

def replica_attention(query_rows, key_rows, value_rows, seg_rows, used_len):
    groups = QH // KVH
    block_count = query_rows.shape[0] // TOK_DEV
    padded_keys = jnp.concatenate([jnp.zeros((3 * TOK_DEV, KVH * HD), key_rows.dtype), key_rows], axis=0)
    padded_values = jnp.concatenate([jnp.zeros((3 * TOK_DEV, KVH * HD), value_rows.dtype), value_rows], axis=0)
    padded_segs = jnp.concatenate([jnp.full((3 * TOK_DEV,), -1, jnp.int32), seg_rows.astype(jnp.int32)], axis=0)

    def one_block(block_index):
        begin = (block_index * TOK_DEV).astype(jnp.int32)
        query_blk = lax.dynamic_slice_in_dim(query_rows, begin, TOK_DEV, 0).astype(jnp.float32)
        key_blk = lax.dynamic_slice_in_dim(padded_keys, begin, 4 * TOK_DEV, 0).astype(jnp.float32)
        value_blk = lax.dynamic_slice_in_dim(padded_values, begin, 4 * TOK_DEV, 0).astype(jnp.float32)
        seg_keys = lax.dynamic_slice_in_dim(padded_segs, begin, 4 * TOK_DEV, 0)
        seg_query = lax.dynamic_slice_in_dim(seg_rows.astype(jnp.int32), begin, TOK_DEV, 0)
        query_pos = begin + jnp.arange(TOK_DEV, dtype=jnp.int32)
        key_pos = begin - 3 * TOK_DEV + jnp.arange(4 * TOK_DEV, dtype=jnp.int32)
        allowed = (seg_query[:, None] == seg_keys[None, :]) & (key_pos[None, :] <= query_pos[:, None])
        query_heads = query_blk.reshape(TOK_DEV, KVH, groups, HD)
        key_heads = key_blk.reshape(4 * TOK_DEV, KVH, HD)
        value_heads = value_blk.reshape(4 * TOK_DEV, KVH, HD)
        scores = jnp.einsum('qhgd,khd->hgqk', query_heads, key_heads) * HD ** (-0.5)
        scores = jnp.where(allowed, scores, -jnp.inf)
        row_max = lax.optimization_barrier(jnp.max(scores, axis=-1, keepdims=True))
        weights = jnp.where(allowed, jnp.exp(scores - row_max), 0.0)
        totals = lax.optimization_barrier(jnp.sum(weights, axis=-1, keepdims=True))
        rounded = weights.astype(jnp.bfloat16)
        rounded = lax.optimization_barrier(rounded).astype(jnp.float32)
        mixed_out = jnp.einsum('hgqk,khd->qhgd', rounded, value_heads)
        mixed_out = mixed_out / jnp.transpose(totals, (2, 0, 1, 3))
        mixed_out = mixed_out.reshape(TOK_DEV, QH * HD)
        query_live = query_pos < used_len
        return jnp.where(query_live[:, None], mixed_out, 0.0).astype(jnp.bfloat16)
    blocks_out = lax.map(one_block, jnp.arange(block_count, dtype=jnp.int32))
    return blocks_out.reshape(block_count * TOK_DEV, QH * HD)

def reference(grad_parts, master_weight, moment_one, moment_two, queries, keys_in, hidden, segment_ids, packed_len):
    grad_total = lax.optimization_barrier(jnp.sum(grad_parts.astype(jnp.float32).reshape(N_DP, D, C), axis=0))
    new_first = beta_one * moment_one + (1.0 - beta_one) * grad_total
    new_second = beta_two * moment_two + (1.0 - beta_two) * grad_total * grad_total
    step_dir = new_first / bias_one / (jnp.sqrt(new_second / bias_two) + adam_eps) + weight_decay * master_weight
    new_master = master_weight - learn_rate * step_dir
    rollout_weight = new_master.astype(jnp.bfloat16)

    def per_replica(replica_items):
        query_rows, key_rows, hidden_rows, seg_rows, used_len = replica_items
        value_rows = jnp.dot(hidden_rows, rollout_weight, preferred_element_type=jnp.float32).astype(jnp.bfloat16)
        return replica_attention(query_rows, key_rows, value_rows, seg_rows, used_len)
    attended = lax.map(per_replica, (queries, keys_in, hidden, segment_ids, packed_len))
    return (new_master, new_first, new_second, attended)
```

```python
import jax
import jax.numpy as jnp
from jax import lax
from jax.experimental import pallas as pl
from jax.experimental.pallas import tpu as pltpu
from jax.sharding import PartitionSpec as P

HD = 128
ALL = ("dp", "replica")

beta_one = 0.9
beta_two = 0.95
bias_one = 1.0 - 0.9**10
bias_two = 1.0 - 0.95**10
adam_eps = 1e-08
learn_rate = 0.002
weight_decay = 0.1


def bits_of(count):
    return [1 << j for j in range(count.bit_length() - 1)]


def swapped(block, mask):
    total = lax.axis_size("dp") * lax.axis_size("replica")
    return lax.ppermute(block, ALL, [(i, i ^ mask) for i in range(total)])


def passed_along(block, distance):
    devices = range(lax.axis_size("dp"))
    route = [(i - distance, i) for i in devices if i - distance in devices]
    return lax.ppermute(block, "dp", route)


def adam_update(grad_sum, master, moment_first, moment_second):
    first_new = beta_one * moment_first + (1.0 - beta_one) * grad_sum
    second_new = beta_two * moment_second + (1.0 - beta_two) * grad_sum * grad_sum
    step_dir = (
        first_new / bias_one / (jnp.sqrt(second_new / bias_two) + adam_eps) + weight_decay * master
    )
    master_new = master - learn_rate * step_dir
    return (master_new, first_new, second_new)


def summed_to_owner(terms, order):
    n_dp, rows, columns = terms.shape
    names = bits_of(n_dp)[::-1]
    me = lax.axis_index("dp")
    n_replica = lax.axis_size("replica")
    held = terms.reshape((2,) * len(names) + (rows, columns))
    for step, bit in enumerate(order):
        axis = names.index(bit)
        names = names[:axis] + names[axis + 1 :]
        mine = (me // bit) % 2
        away = lax.dynamic_index_in_dim(held, 1 - mine, axis, keepdims=False)
        kept = lax.dynamic_index_in_dim(held, mine, axis, keepdims=False)
        came = swapped(away, bit * n_replica)
        held = kept.astype(jnp.float32) + came.astype(jnp.float32)
        if step < len(order) - 1:
            held = held.astype(jnp.bfloat16)
    return held


def gathered(rows, order):
    n_replica = lax.axis_size("replica")
    held, labels = rows, [0]
    for bit in order[:-1]:
        held = jnp.concatenate([held, swapped(held, bit * n_replica)], axis=0)
        labels = labels + [label ^ bit for label in labels]
    last = swapped(held, order[-1] * n_replica)
    return held, last, labels + [label ^ order[-1] for label in labels]


def packed_columns(hidden_rows, picks, width):
    tokens = hidden_rows.shape[0]
    offsets, blocks = picks.shape
    if width % HD:
        cut = hidden_rows.reshape(tokens, -1, width)
        taken = jnp.take(cut, picks.reshape(-1), axis=1).reshape(tokens, offsets, blocks * width)
        return jnp.transpose(taken, (1, 0, 2))

    def kernel(picks_ref, source_ref, out_ref, sems):
        copies = []
        for m in range(offsets):
            for o in range(blocks):
                start = pl.multiple_of(picks_ref[m, o] * width, width)
                copies.append(
                    pltpu.make_async_copy(
                        source_ref.at[:, pl.ds(start, width)],
                        out_ref.at[m, :, pl.ds(o * width, width)],
                        sems.at[m, o],
                    )
                )
        for copy in copies:
            copy.start()
        for copy in copies:
            copy.wait()

    return pl.pallas_call(
        kernel,
        out_shape=jax.ShapeDtypeStruct((offsets, tokens, blocks * width), hidden_rows.dtype),
        in_specs=[
            pl.BlockSpec(memory_space=pltpu.SMEM),
            pl.BlockSpec(memory_space=pl.ANY),
        ],
        out_specs=pl.BlockSpec(memory_space=pl.ANY),
        scratch_shapes=[pltpu.SemaphoreType.DMA((offsets, blocks))],
        cost_estimate=pl.CostEstimate(
            flops=0, bytes_accessed=4 * hidden_rows.size, transcendentals=0
        ),
        name="pack_hidden",
    )(picks, hidden_rows)


def attention_weights(place, queries, seg_column, key_blocks):
    tokens = queries.shape[1]
    heads_kv = key_blocks[0].shape[1] // HD
    groups = queries.shape[2] // (heads_kv * HD)
    spans = len(key_blocks)
    padded = key_blocks[0].shape[0]
    keys_all = spans * tokens

    def kernel(place_ref, q_ref, seg_ref, *rest):
        key_refs, out_ref = rest[:-1], rest[-1]
        here, used = place_ref[0], place_ref[1]
        keys = jnp.concatenate([ref[0:tokens, :] for ref in key_refs], axis=0)
        seg_keys = jnp.concatenate(
            [ref[tokens : tokens + 16, :].astype(jnp.float32)[0:1, :] for ref in key_refs], axis=1
        )
        row = lax.broadcasted_iota(jnp.int32, (tokens, keys_all), 0)
        column = lax.broadcasted_iota(jnp.int32, (tokens, keys_all), 1)
        offset = column - (spans - 1) * tokens
        allowed = (
            (seg_ref[...] == seg_keys) & (offset <= row) & (offset + here * tokens >= 0)
        )
        live = (here * tokens + lax.broadcasted_iota(jnp.int32, (tokens, 1), 0)) < used
        for j in range(groups):
            scores = lax.dot_general(
                q_ref[0, :, j * HD : (j + 1) * HD],
                keys,
                (((1,), (1,)), ((), ())),
                preferred_element_type=jnp.float32,
            ) * HD ** (-0.5)
            scores = jnp.where(allowed, scores, -1e30)
            weights = jnp.exp(scores - jnp.max(scores, axis=-1, keepdims=True))
            totals = jnp.sum(weights, axis=-1, keepdims=True)
            scale = jnp.where(live, 1.0 / totals, 0.0)
            out_ref[0, j * tokens : (j + 1) * tokens, :] = (weights * scale).astype(jnp.bfloat16)

    key_spec = pl.BlockSpec((padded, HD), lambda g: (0, g))
    return pl.pallas_call(
        kernel,
        grid=(heads_kv,),
        out_shape=jax.ShapeDtypeStruct((heads_kv, groups * tokens, keys_all), jnp.bfloat16),
        in_specs=[
            pl.BlockSpec(memory_space=pltpu.SMEM),
            pl.BlockSpec((1, tokens, groups * HD), lambda g: (0, 0, g)),
            pl.BlockSpec((tokens, 1), lambda g: (0, 0)),
        ]
        + [key_spec] * spans,
        out_specs=pl.BlockSpec((1, groups * tokens, keys_all), lambda g: (g, 0, 0)),
        cost_estimate=pl.CostEstimate(
            flops=2 * heads_kv * groups * tokens * keys_all * HD,
            bytes_accessed=2 * heads_kv * groups * tokens * (keys_all + HD),
            transcendentals=heads_kv * groups * tokens * keys_all,
        ),
        name="attention_weights",
    )(place, queries, seg_column, *key_blocks)


def weighted_values(weights, value_parts):
    heads_kv, rows, keys_all = weights.shape
    spans = len(value_parts[0])
    tokens = keys_all // spans
    groups = rows // tokens
    part_heads = value_parts[0][0].shape[1] // HD
    parts = len(value_parts)

    def kernel(w_ref, *rest):
        value_refs, out_ref = rest[:-1], rest[-1]
        g = pl.program_id(0)
        for part in range(parts):

            @pl.when(g // part_heads == part)
            def _():
                refs = value_refs[part * spans : (part + 1) * spans]
                values = jnp.concatenate([ref[...] for ref in refs], axis=0)
                mixed = jnp.dot(w_ref[0], values, preferred_element_type=jnp.float32)
                for j in range(groups):
                    out_ref[0, :, j * HD : (j + 1) * HD] = mixed[
                        j * tokens : (j + 1) * tokens, :
                    ].astype(jnp.bfloat16)

    in_specs = [pl.BlockSpec((1, rows, keys_all), lambda g: (g, 0, 0))]
    for _ in range(parts * spans):
        in_specs.append(pl.BlockSpec((tokens, HD), lambda g: (0, g % part_heads)))
    return pl.pallas_call(
        kernel,
        grid=(heads_kv,),
        out_shape=jax.ShapeDtypeStruct((1, tokens, heads_kv * groups * HD), jnp.bfloat16),
        in_specs=in_specs,
        out_specs=pl.BlockSpec((1, tokens, groups * HD), lambda g: (0, 0, g)),
        cost_estimate=pl.CostEstimate(
            flops=2 * heads_kv * rows * keys_all * HD,
            bytes_accessed=2 * heads_kv * rows * keys_all,
            transcendentals=0,
        ),
        name="weighted_values",
    )(weights, *[block for part in value_parts for block in part])


def on_device(
    grad_parts,
    master_weight,
    moment_one,
    moment_two,
    queries,
    keys_in,
    hidden,
    segment_ids,
    packed_len,
):
    n_dp, n_replica = lax.axis_size("dp"), lax.axis_size("replica")
    dp, replica = lax.axis_index("dp"), lax.axis_index("replica")
    tokens = queries.shape[1]
    rows, columns = master_weight.shape
    half = columns // 2
    bits = bits_of(n_dp)
    orders = [bits, [bits[1], bits[0]] + bits[2:]]

    first_parts = []
    sums = []
    for part, order in enumerate(orders):
        sums.append(summed_to_owner(grad_parts[:, :, part * half : (part + 1) * half], order))
    new_master, new_first, new_second = adam_update(
        jnp.concatenate(sums, axis=1), master_weight, moment_one, moment_two
    )
    weight_parts = []
    for part, order in enumerate(orders):
        cut = slice(part * half, (part + 1) * half)
        updated = adam_update(
            sums[part], master_weight[:, cut], moment_one[:, cut], moment_two[:, cut]
        )[0].astype(jnp.bfloat16)
        weight_parts.append(gathered(updated, order[::-1]))

    labels = weight_parts[0][2]
    assert sorted(labels) == list(range(n_dp))
    owner = dp ^ jnp.arange(n_dp, dtype=jnp.int32)
    offsets = jnp.arange(n_replica, dtype=jnp.int32)
    picks = owner[None, :] * n_replica + (replica ^ offsets)[:, None]
    packed = packed_columns(hidden[0], picks, rows)
    token_rows = [packed[0]] + [swapped(packed[m], m) for m in range(1, n_replica)]
    token_rows = jnp.concatenate(token_rows, axis=0)

    seg_row = jnp.tile(segment_ids.astype(jnp.bfloat16), (16, columns // tokens))
    key_own = jnp.concatenate([keys_in[0], seg_row], axis=0)
    key_blocks = [passed_along(key_own, d) for d in (3, 2, 1)] + [key_own]
    place = jnp.stack([dp.astype(jnp.int32), packed_len[0]])
    seg_column = segment_ids.astype(jnp.float32).reshape(tokens, 1)
    weights = attention_weights(place, queries, seg_column, key_blocks)

    value_parts = []
    for held, last, labels in weight_parts:
        early = len(labels) // 2

        def columns_of(picked):
            return jnp.concatenate(
                [token_rows[:, o * rows : (o + 1) * rows] for o in picked], axis=1
            )

        partial = jnp.dot(
            columns_of(labels[:early]), held, preferred_element_type=jnp.float32
        ) + jnp.dot(columns_of(labels[early:]), last, preferred_element_type=jnp.float32)
        partial = partial.reshape(n_replica, tokens, half)
        for bit in bits_of(n_replica):
            partial = partial.reshape(-1, 2, tokens, half)
            came = swapped(partial[:, 1].astype(jnp.bfloat16), bit)
            partial = partial[:, 0] + came.astype(jnp.float32)
        value = partial[0].astype(jnp.bfloat16)
        value_parts.append([passed_along(value, d) for d in (3, 2, 1)] + [value])
    attended = weighted_values(weights, value_parts)
    return (new_master, new_first, new_second, attended)


def solution(mesh):
    in_specs = (
        P("dp", "replica", None),
        P(("dp", "replica"), None),
        P(("dp", "replica"), None),
        P(("dp", "replica"), None),
        P("replica", "dp", None),
        P("replica", "dp", None),
        P("replica", "dp", None),
        P("replica", "dp"),
        P("replica"),
    )
    out_specs = (
        P(("dp", "replica"), None),
        P(("dp", "replica"), None),
        P(("dp", "replica"), None),
        P("replica", "dp", None),
    )
    return jax.shard_map(
        on_device, mesh=mesh, in_specs=in_specs, out_specs=out_specs, check_vma=False
    )
```

```python
import jax
import jax.numpy as jnp
from jax import lax
from jax.experimental import pallas as pl
from jax.experimental.pallas import tpu as pltpu
from jax.sharding import PartitionSpec as P

HD = 128
ALL = ("dp", "replica")
STREAMS = 2

beta_one = 0.9
beta_two = 0.95
bias_one = 1.0 - 0.9**10
bias_two = 1.0 - 0.95**10
adam_eps = 1e-08
learn_rate = 0.002
weight_decay = 0.1


def bits_of(count):
    return [1 << j for j in range(count.bit_length() - 1)]


def swapped(block, mask):
    total = lax.axis_size("dp") * lax.axis_size("replica")
    return lax.ppermute(block, ALL, [(i, i ^ mask) for i in range(total)])


def passed_along(block, distance):
    n_dp = lax.axis_size("dp")
    return lax.ppermute(block, "dp", [(i, (i + distance) % n_dp) for i in range(n_dp)])


def adam_update(grad_sum, master, moment_first, moment_second):
    first_new = beta_one * moment_first + (1.0 - beta_one) * grad_sum
    second_new = beta_two * moment_second + (1.0 - beta_two) * grad_sum * grad_sum
    step_dir = (
        first_new / bias_one / (jnp.sqrt(second_new / bias_two) + adam_eps) + weight_decay * master
    )
    master_new = master - learn_rate * step_dir
    return (master_new, first_new, second_new)


def tied(*values):
    return lax.optimization_barrier(values)


def packed_columns(hidden_rows, picks, width):
    tokens = hidden_rows.shape[0]
    offsets, blocks = picks.shape
    if width % HD:
        cut = hidden_rows.reshape(tokens, -1, width)
        taken = jnp.take(cut, picks.reshape(-1), axis=1).reshape(tokens, offsets, blocks * width)
        return [taken[:, m] for m in range(offsets)]

    def kernel(picks_ref, source_ref, *out_refs):
        for m in range(offsets):
            for o in range(blocks):
                start = pl.multiple_of(picks_ref[m, o] * width, width)
                out_refs[m][:, o * width : (o + 1) * width] = source_ref[:, pl.ds(start, width)]

    return pl.pallas_call(
        kernel,
        out_shape=[
            jax.ShapeDtypeStruct((tokens, blocks * width), hidden_rows.dtype)
            for _ in range(offsets)
        ],
        in_specs=[
            pl.BlockSpec(memory_space=pltpu.SMEM),
            pl.BlockSpec(memory_space=pltpu.VMEM),
        ],
        out_specs=[pl.BlockSpec(memory_space=pltpu.VMEM)] * offsets,
        compiler_params=pltpu.CompilerParams(vmem_limit_bytes=16 * 2**20),
        cost_estimate=pl.CostEstimate(
            flops=0, bytes_accessed=4 * hidden_rows.size, transcendentals=0
        ),
        name="pack_hidden",
    )(picks, hidden_rows)


def projected(token_blocks, pieces, width, before):
    count = len(token_blocks)
    tokens = token_blocks[0].shape[0]
    columns = pieces[0][0].shape[1]
    depth = sum(piece.shape[0] for piece, _ in pieces)

    def total_of(token_ref, weight_refs):
        total = None
        for weight_ref, (_, places) in zip(weight_refs, pieces):
            for i, place in enumerate(places):
                term = jnp.dot(
                    token_ref[:, place * width : (place + 1) * width],
                    weight_ref[i * width : (i + 1) * width, :],
                    preferred_element_type=jnp.float32,
                )
                total = term if total is None else total + term
        return total

    def first_kernel(*refs):
        for m in range(count):
            refs[-1][m] = total_of(refs[m], refs[count:-1])

    def last_kernel(*refs):
        kept_ref, away_ref = refs[-2], refs[-1]
        for m in range(count):
            total = refs[count][m] + total_of(refs[m], refs[count + 1 : -2])
            if m % 2:
                away_ref[m // 2] = total.astype(jnp.bfloat16)
            else:
                kept_ref[m // 2] = total

    cost = pl.CostEstimate(
        flops=2 * count * tokens * depth * columns,
        bytes_accessed=2 * count * tokens * depth,
        transcendentals=0,
    )
    params = pltpu.CompilerParams(vmem_limit_bytes=24 * 2**20)
    weights = [piece for piece, _ in pieces]
    if before is None:
        return pl.pallas_call(
            first_kernel,
            out_shape=jax.ShapeDtypeStruct((count, tokens, columns), jnp.float32),
            compiler_params=params,
            cost_estimate=cost,
            name="projected_first",
        )(*token_blocks, *weights)
    return pl.pallas_call(
        last_kernel,
        out_shape=(
            jax.ShapeDtypeStruct((count // 2, tokens, columns), jnp.float32),
            jax.ShapeDtypeStruct((count // 2, tokens, columns), jnp.bfloat16),
        ),
        compiler_params=params,
        cost_estimate=cost,
        name="projected_last",
    )(*token_blocks, before, *weights)


def attention_weights(place, queries, seg_column, key_blocks):
    tokens = queries.shape[1]
    heads_kv = key_blocks[0].shape[1] // HD
    groups = queries.shape[2] // (heads_kv * HD)
    spans = len(key_blocks)
    padded = key_blocks[0].shape[0]
    keys_all = spans * tokens

    def kernel(place_ref, q_ref, seg_ref, *rest):
        key_refs, out_ref = rest[:-1], rest[-1]
        here, used = place_ref[0], place_ref[1]
        keys = jnp.concatenate([ref[0:tokens, :] for ref in key_refs], axis=0)
        seg_keys = jnp.concatenate(
            [ref[tokens : tokens + 16, :].astype(jnp.float32)[0:1, :] for ref in key_refs], axis=1
        )
        row = lax.broadcasted_iota(jnp.int32, (tokens, keys_all), 0)
        column = lax.broadcasted_iota(jnp.int32, (tokens, keys_all), 1)
        offset = column - (spans - 1) * tokens
        allowed = (
            (seg_ref[...] == seg_keys) & (offset <= row) & (offset + here * tokens >= 0)
        )
        live = (here * tokens + lax.broadcasted_iota(jnp.int32, (tokens, 1), 0)) < used
        for j in range(groups):
            scores = lax.dot_general(
                q_ref[0, :, j * HD : (j + 1) * HD],
                keys,
                (((1,), (1,)), ((), ())),
                preferred_element_type=jnp.float32,
            ) * HD ** (-0.5)
            scores = jnp.where(allowed, scores, -1e30)
            weights = jnp.exp(scores - jnp.max(scores, axis=-1, keepdims=True))
            totals = jnp.sum(weights, axis=-1, keepdims=True)
            scale = jnp.where(live, 1.0 / totals, 0.0)
            out_ref[0, j * tokens : (j + 1) * tokens, :] = (weights * scale).astype(jnp.bfloat16)

    key_spec = pl.BlockSpec((padded, HD), lambda g: (0, g))
    return pl.pallas_call(
        kernel,
        grid=(heads_kv,),
        out_shape=jax.ShapeDtypeStruct((heads_kv, groups * tokens, keys_all), jnp.bfloat16),
        in_specs=[
            pl.BlockSpec(memory_space=pltpu.SMEM),
            pl.BlockSpec((1, tokens, groups * HD), lambda g: (0, 0, g)),
            pl.BlockSpec((tokens, 1), lambda g: (0, 0)),
        ]
        + [key_spec] * spans,
        out_specs=pl.BlockSpec((1, groups * tokens, keys_all), lambda g: (g, 0, 0)),
        cost_estimate=pl.CostEstimate(
            flops=2 * heads_kv * groups * tokens * keys_all * HD,
            bytes_accessed=2 * heads_kv * groups * tokens * (keys_all + HD),
            transcendentals=heads_kv * groups * tokens * keys_all,
        ),
        name="attention_weights",
    )(place, queries, seg_column, *key_blocks)


def weighted_values(weights, value_blocks):
    heads_kv, rows, keys_all = weights.shape
    tokens, columns = value_blocks[0].shape
    groups = rows // tokens

    def kernel(w_ref, *rest):
        value_refs, out_ref = rest[:-1], rest[-1]
        values = jnp.concatenate([ref[...] for ref in value_refs], axis=0)
        mixed = jnp.dot(w_ref[0], values, preferred_element_type=jnp.float32)
        for j in range(groups):
            out_ref[0, :, j * HD : (j + 1) * HD] = mixed[j * tokens : (j + 1) * tokens, :].astype(
                jnp.bfloat16
            )

    return pl.pallas_call(
        kernel,
        grid=(heads_kv,),
        out_shape=jax.ShapeDtypeStruct((1, tokens, heads_kv * groups * HD), jnp.bfloat16),
        in_specs=[pl.BlockSpec((1, rows, keys_all), lambda g: (g, 0, 0))]
        + [pl.BlockSpec((tokens, HD), lambda g: (0, g))] * len(value_blocks),
        out_specs=pl.BlockSpec((1, tokens, groups * HD), lambda g: (0, 0, g)),
        compiler_params=pltpu.CompilerParams(vmem_limit_bytes=16 * 2**20),
        cost_estimate=pl.CostEstimate(
            flops=2 * heads_kv * rows * keys_all * HD,
            bytes_accessed=2 * heads_kv * rows * keys_all,
            transcendentals=0,
        ),
        name="weighted_values",
    )(weights, *value_blocks)


def on_device(
    grad_parts,
    master_weight,
    moment_one,
    moment_two,
    queries,
    keys_in,
    hidden,
    segment_ids,
    packed_len,
):
    n_dp, n_replica = lax.axis_size("dp"), lax.axis_size("replica")
    dp, replica = lax.axis_index("dp"), lax.axis_index("replica")
    tokens = queries.shape[1]
    rows, columns = master_weight.shape
    bits = bits_of(n_dp)
    orders = [bits, [bits[1], bits[0]] + bits[2:]] * (STREAMS // 2)
    width = columns // STREAMS
    cuts = [slice(part * width, (part + 1) * width) for part in range(STREAMS)]
    steps = len(bits)

    owner = dp ^ jnp.arange(n_dp, dtype=jnp.int32)
    offsets = jnp.arange(n_replica, dtype=jnp.int32)
    picks = owner[None, :] * n_replica + (replica ^ offsets)[:, None]

    seg_row = jnp.tile(segment_ids.astype(jnp.bfloat16), (16, columns // tokens))
    key_own = jnp.concatenate([keys_in[0], seg_row], axis=0)
    place = jnp.stack([dp.astype(jnp.int32), packed_len[0]])
    seg_column = segment_ids.astype(jnp.float32).reshape(tokens, 1)

    names = bits[::-1]
    held = [
        grad_parts[:, :, cut].reshape((2,) * len(names) + (rows, width)) for cut in cuts
    ]
    axes = [list(names) for _ in cuts]
    for step in range(steps):
        came = []
        for part, order in enumerate(orders):
            bit = order[step]
            axis = axes[part].index(bit)
            axes[part].pop(axis)
            mine = (dp // bit) % 2
            leaving = lax.dynamic_index_in_dim(held[part], 1 - mine, axis, keepdims=False)
            held[part] = lax.dynamic_index_in_dim(held[part], mine, axis, keepdims=False)
            came.append(swapped(leaving, bit * n_replica))
        if step == 0:
            packed = packed_columns(hidden[0], picks, rows)
            came[0], *packed = tied(came[0], *packed)
            token_blocks = [packed[0]] + [swapped(packed[m], m) for m in range(1, n_replica)]
        if step == 1:
            came[0], token_blocks[2] = tied(came[0], token_blocks[2])
            key_blocks = [passed_along(key_own, d) for d in (3, 2, 1)] + [key_own]
        for part in range(STREAMS):
            held[part] = held[part].astype(jnp.float32) + came[part].astype(jnp.float32)
            if step < steps - 1:
                held[part] = held[part].astype(jnp.bfloat16)

    fresh = []
    labels = [[0] for _ in cuts]
    for part, cut in enumerate(cuts):
        updated = adam_update(
            held[part], master_weight[:, cut], moment_one[:, cut], moment_two[:, cut]
        )
        fresh.append(updated[0].astype(jnp.bfloat16))
    new_master, new_first, new_second = adam_update(
        jnp.concatenate(held, axis=1), master_weight, moment_one, moment_two
    )
    for step in range(steps):
        came = [
            swapped(rows_here, order[-1 - step] * n_replica)
            for rows_here, order in zip(fresh, orders)
        ]
        if step == 0:
            came[0], *token_blocks = tied(came[0], *token_blocks)
        if step == 1:
            came[1], *key_blocks = tied(came[1], *key_blocks)
            weights = attention_weights(place, queries, seg_column, key_blocks)
        if step == steps - 1:
            came[0], weights = tied(came[0], weights)
            break
        for part, order in enumerate(orders):
            fresh[part] = jnp.concatenate([fresh[part], came[part]], axis=0)
            labels[part] = labels[part] + [label ^ order[-1 - step] for label in labels[part]]

    sent = []
    for part, order in enumerate(orders):
        before = projected(token_blocks, [(fresh[part], labels[part])], rows, None)
        last = [label ^ order[0] for label in labels[part]]
        kept, leaving = projected(token_blocks, [(came[part], last)], rows, before)
        sent.append(kept + swapped(leaving, 1).astype(jnp.float32))
    partial = jnp.concatenate(sent, axis=2)
    for bit in bits_of(n_replica)[1:]:
        partial = partial.reshape(-1, 2, tokens, columns)
        came = swapped(partial[:, 1].astype(jnp.bfloat16), bit)
        partial = partial[:, 0] + came.astype(jnp.float32)
    value = partial[0].astype(jnp.bfloat16)
    value_blocks = [passed_along(value, d) for d in (3, 2, 1)] + [value]
    attended = weighted_values(weights, value_blocks)
    return (new_master, new_first, new_second, attended)


def solution(mesh):
    in_specs = (
        P("dp", "replica", None),
        P(("dp", "replica"), None),
        P(("dp", "replica"), None),
        P(("dp", "replica"), None),
        P("replica", "dp", None),
        P("replica", "dp", None),
        P("replica", "dp", None),
        P("replica", "dp"),
        P("replica"),
    )
    out_specs = (
        P(("dp", "replica"), None),
        P(("dp", "replica"), None),
        P(("dp", "replica"), None),
        P("replica", "dp", None),
    )
    return jax.shard_map(
        on_device, mesh=mesh, in_specs=in_specs, out_specs=out_specs, check_vma=False
    )
```

```python
import jax
import jax.numpy as jnp
from jax import lax
from jax.experimental import pallas as pl
from jax.experimental.pallas import tpu as pltpu
from jax.sharding import PartitionSpec as P

HD = 128
ALL = ("dp", "replica")
SMALL = 12 * 2**20

beta_one = 0.9
beta_two = 0.95
bias_one = 1.0 - 0.9**10
bias_two = 1.0 - 0.95**10
adam_eps = 1e-08
learn_rate = 0.002
weight_decay = 0.1


def bits_of(count):
    return [1 << j for j in range(count.bit_length() - 1)]


def swapped(block, mask):
    total = lax.axis_size("dp") * lax.axis_size("replica")
    return lax.ppermute(block, ALL, [(i, i ^ mask) for i in range(total)])


def passed_along(block, distance):
    n_dp = lax.axis_size("dp")
    return lax.ppermute(block, "dp", [(i, i + distance) for i in range(n_dp - distance)])


def adam_update(grad_sum, master, moment_first, moment_second):
    first_new = beta_one * moment_first + (1.0 - beta_one) * grad_sum
    second_new = beta_two * moment_second + (1.0 - beta_two) * grad_sum * grad_sum
    step_dir = (
        first_new / bias_one / (jnp.sqrt(second_new / bias_two) + adam_eps) + weight_decay * master
    )
    master_new = master - learn_rate * step_dir
    return (master_new, first_new, second_new)


def tied(*values):
    return lax.optimization_barrier(values)


def halving(bits):
    if not bits:
        return [0]
    rest = halving(bits[1:])
    return [offset | bits[0] for offset in rest] + rest


def blocks_taken(terms, flips):
    _, rows, columns = terms.shape
    parts, blocks = len(flips), len(flips[0])
    width = columns // parts

    def kernel(terms_ref, *refs):
        out_refs, sems = refs[:parts], refs[parts]
        here = lax.axis_index("dp")
        copies = []
        for part in range(parts):
            for i, flip in enumerate(flips[part]):
                copies.append(
                    pltpu.make_async_copy(
                        terms_ref.at[here ^ flip, :, pl.ds(part * width, width)],
                        out_refs[part].at[i],
                        sems.at[part, i],
                    )
                )
        for copy in copies:
            copy.start()
        for copy in copies:
            copy.wait()

    return pl.pallas_call(
        kernel,
        in_specs=[pl.BlockSpec(memory_space=pltpu.HBM)],
        out_specs=[pl.BlockSpec(memory_space=pltpu.VMEM)] * parts,
        out_shape=[jax.ShapeDtypeStruct((blocks, rows, width), terms.dtype)] * parts,
        scratch_shapes=[pltpu.SemaphoreType.DMA((parts, blocks))],
        compiler_params=pltpu.CompilerParams(vmem_limit_bytes=SMALL),
        cost_estimate=pl.CostEstimate(
            flops=0, bytes_accessed=4 * blocks * rows * columns, transcendentals=0
        ),
        name="blocks_taken",
    )(terms)


def first_half_sums(streams, left):
    count = len(streams)
    sizes = [len(terms) for terms in streams]
    _, rows, width = streams[0][0].shape

    def kernel(*refs):
        out_ref = refs[-1]
        at = 0
        for i, size in enumerate(sizes):
            for j in range(left // 2):
                total = None
                for ref in refs[at : at + size]:
                    term = ref[ref.shape[0] - left + j].astype(jnp.float32)
                    total = term if total is None else total + term
                out_ref[i, j] = total.astype(jnp.bfloat16)
            at += size

    out = jax.ShapeDtypeStruct((count, left // 2, rows, width), jnp.bfloat16)
    return pl.pallas_call(
        kernel,
        out_shape=out,
        compiler_params=pltpu.CompilerParams(vmem_limit_bytes=SMALL),
        cost_estimate=pl.CostEstimate(
            flops=2 * sizes[0] * out.size, bytes_accessed=8 * out.size, transcendentals=0
        ),
        name="first_half_sums",
    )(*[term for terms in streams for term in terms])


def fresh_rows(streams, state):
    parts = len(streams)
    sizes = [len(terms) for terms in streams]
    _, rows, width = streams[0][0].shape

    def kernel(*refs):
        master_ref, first_ref, second_ref, out_ref = refs[-4:]
        at = 0
        for part, size in enumerate(sizes):
            grad = None
            for ref in refs[at : at + size]:
                term = ref[ref.shape[0] - 1].astype(jnp.float32)
                grad = term if grad is None else grad + term
            at += size
            cut = slice(part * width, (part + 1) * width)
            updated = adam_update(grad, master_ref[:, cut], first_ref[:, cut], second_ref[:, cut])
            out_ref[part] = updated[0].astype(jnp.bfloat16)

    out = jax.ShapeDtypeStruct((parts, rows, width), jnp.bfloat16)
    return pl.pallas_call(
        kernel,
        out_shape=out,
        compiler_params=pltpu.CompilerParams(vmem_limit_bytes=SMALL),
        cost_estimate=pl.CostEstimate(
            flops=20 * out.size, bytes_accessed=20 * out.size, transcendentals=out.size
        ),
        name="fresh_rows",
    )(*[term for terms in streams for term in terms], *state)


def one_below(first, second, part=None):
    rows, width = first.shape[-2:]

    def kernel(first_ref, second_ref, out_ref):
        out_ref[:rows] = first_ref[...] if part is None else first_ref[part]
        out_ref[rows:] = second_ref[...] if part is None else second_ref[part]

    return pl.pallas_call(
        kernel,
        out_shape=jax.ShapeDtypeStruct((2 * rows, width), first.dtype),
        compiler_params=pltpu.CompilerParams(vmem_limit_bytes=SMALL),
        cost_estimate=pl.CostEstimate(
            flops=0, bytes_accessed=8 * rows * width, transcendentals=0
        ),
        name="one_below",
    )(first, second)


def staged(arrays):
    count = len(arrays)

    def kernel(*refs):
        for i in range(count):
            refs[count + i][...] = refs[i][...]

    rows, columns = arrays[0].shape
    return pl.pallas_call(
        kernel,
        grid=(2,),
        in_specs=[pl.BlockSpec((rows, columns // 2), lambda i: (0, i))] * count,
        out_specs=[pl.BlockSpec((rows, columns // 2), lambda i: (0, i))] * count,
        out_shape=[jax.ShapeDtypeStruct(x.shape, x.dtype) for x in arrays],
        compiler_params=pltpu.CompilerParams(vmem_limit_bytes=SMALL),
        cost_estimate=pl.CostEstimate(
            flops=0, bytes_accessed=8 * count * arrays[0].size, transcendentals=0
        ),
        name="staged",
    )(*arrays)


def packed_columns(hidden_rows, width, n_dp, n_replica):
    tokens = hidden_rows.shape[0]
    if width % HD:
        owner = lax.axis_index("dp") ^ jnp.arange(n_dp, dtype=jnp.int32)
        replica = lax.axis_index("replica") ^ jnp.arange(n_replica, dtype=jnp.int32)
        picks = owner[None, :] * n_replica + replica[:, None]
        cut = hidden_rows.reshape(tokens, -1, width)
        taken = jnp.take(cut, picks.reshape(-1), axis=1)
        taken = taken.reshape(tokens, n_replica, n_dp * width)
        return [taken[:, m] for m in range(n_replica)]

    def kernel(source_ref, *out_refs):
        dp, replica = lax.axis_index("dp"), lax.axis_index("replica")
        for m in range(n_replica):
            for o in range(n_dp):
                start = pl.multiple_of(((dp ^ o) * n_replica + (replica ^ m)) * width, width)
                out_refs[m][:, o * width : (o + 1) * width] = source_ref[:, pl.ds(start, width)]

    return pl.pallas_call(
        kernel,
        out_shape=[
            jax.ShapeDtypeStruct((tokens, n_dp * width), hidden_rows.dtype)
            for _ in range(n_replica)
        ],
        compiler_params=pltpu.CompilerParams(vmem_limit_bytes=16 * 2**20),
        cost_estimate=pl.CostEstimate(
            flops=0, bytes_accessed=4 * hidden_rows.size, transcendentals=0
        ),
        name="pack_hidden",
    )(hidden_rows)


def projected(token_blocks, pieces, width, before):
    count = len(token_blocks)
    parts = len(pieces)
    tokens = token_blocks[0].shape[0]
    depth, columns = pieces[0][0].shape

    def total_of(token_ref, weight_ref, places):
        total = None
        for i, place in enumerate(places):
            term = jnp.dot(
                token_ref[:, place * width : (place + 1) * width],
                weight_ref[i * width : (i + 1) * width, :],
                preferred_element_type=jnp.float32,
            )
            total = term if total is None else total + term
        return total

    def first_kernel(*refs):
        for m in range(count):
            for part in range(parts):
                total = total_of(refs[m], refs[count + part], pieces[part][1])
                refs[-1][m, :, part * columns : (part + 1) * columns] = total

    def last_kernel(*refs):
        kept_ref, away_ref = refs[-2], refs[-1]
        for m in range(count):
            for part in range(parts):
                cut = slice(part * columns, (part + 1) * columns)
                total = total_of(refs[m], refs[count + 1 + part], pieces[part][1])
                total = refs[count][m, :, cut] + total
                if m % 2:
                    away_ref[m // 2, :, cut] = total.astype(jnp.bfloat16)
                else:
                    kept_ref[m // 2, :, cut] = total

    cost = pl.CostEstimate(
        flops=2 * count * tokens * depth * columns * parts,
        bytes_accessed=2 * count * tokens * depth * parts,
        transcendentals=0,
    )
    params = pltpu.CompilerParams(vmem_limit_bytes=24 * 2**20)
    weights = [piece for piece, _ in pieces]
    if before is None:
        return pl.pallas_call(
            first_kernel,
            out_shape=jax.ShapeDtypeStruct((count, tokens, columns * parts), jnp.float32),
            compiler_params=params,
            cost_estimate=cost,
            name="projected_first",
        )(*token_blocks, *weights)
    return pl.pallas_call(
        last_kernel,
        out_shape=(
            jax.ShapeDtypeStruct((count // 2, tokens, columns * parts), jnp.float32),
            jax.ShapeDtypeStruct((count // 2, tokens, columns * parts), jnp.bfloat16),
        ),
        compiler_params=params,
        cost_estimate=cost,
        name="projected_last",
    )(*token_blocks, before, *weights)


def keys_and_numbers(keys_in, segment_ids):
    _, tokens, columns = keys_in.shape

    def kernel(key_ref, seg_ref, out_ref):
        out_ref[:tokens, :] = key_ref[0]
        numbers = seg_ref[...].astype(jnp.float32)
        numbers = jnp.concatenate([numbers] * (columns // tokens), axis=1)
        out_ref[tokens:, :] = jnp.broadcast_to(numbers, (16, columns)).astype(jnp.bfloat16)

    return pl.pallas_call(
        kernel,
        out_shape=jax.ShapeDtypeStruct((tokens + 16, columns), keys_in.dtype),
        compiler_params=pltpu.CompilerParams(vmem_limit_bytes=SMALL),
        name="keys_and_numbers",
    )(keys_in, segment_ids)


def attention_weights(packed_len, queries, key_blocks):
    tokens = queries.shape[1]
    heads_kv = key_blocks[0].shape[1] // HD
    groups = queries.shape[2] // (heads_kv * HD)
    spans = len(key_blocks)
    padded = key_blocks[0].shape[0]
    keys_all = spans * tokens

    def kernel(used_ref, q_ref, *rest):
        key_refs, out_ref = rest[:-1], rest[-1]
        here, used = lax.axis_index("dp"), used_ref[0]
        keys = jnp.concatenate([ref[0:tokens, :] for ref in key_refs], axis=0)
        seg_keys = jnp.concatenate(
            [ref[tokens : tokens + 16, :].astype(jnp.float32)[0:1, :] for ref in key_refs], axis=1
        )
        row = lax.broadcasted_iota(jnp.int32, (tokens, keys_all), 0)
        offset = lax.broadcasted_iota(jnp.int32, (tokens, keys_all), 1) - (spans - 1) * tokens
        seg_own = jnp.sum(jnp.where(offset == row, seg_keys, 0.0), axis=1, keepdims=True)
        allowed = (seg_own == seg_keys) & (offset <= row) & (offset + here * tokens >= 0)
        live = (here * tokens + lax.broadcasted_iota(jnp.int32, (tokens, 1), 0)) < used
        for j in range(groups):
            scores = lax.dot_general(
                q_ref[0, :, j * HD : (j + 1) * HD],
                keys,
                (((1,), (1,)), ((), ())),
                preferred_element_type=jnp.float32,
            ) * HD ** (-0.5)
            scores = jnp.where(allowed, scores, -1e30)
            weights = jnp.exp(scores - jnp.max(scores, axis=-1, keepdims=True))
            totals = jnp.sum(weights, axis=-1, keepdims=True)
            scale = jnp.where(live, 1.0 / totals, 0.0)
            out_ref[0, j * tokens : (j + 1) * tokens, :] = (weights * scale).astype(jnp.bfloat16)

    key_spec = pl.BlockSpec((padded, HD), lambda g: (0, g))
    return pl.pallas_call(
        kernel,
        grid=(heads_kv,),
        out_shape=jax.ShapeDtypeStruct((heads_kv, groups * tokens, keys_all), jnp.bfloat16),
        in_specs=[
            pl.BlockSpec(memory_space=pltpu.SMEM),
            pl.BlockSpec((1, tokens, groups * HD), lambda g: (0, 0, g)),
        ]
        + [key_spec] * spans,
        out_specs=pl.BlockSpec((1, groups * tokens, keys_all), lambda g: (g, 0, 0)),
        compiler_params=pltpu.CompilerParams(vmem_limit_bytes=16 * 2**20),
        cost_estimate=pl.CostEstimate(
            flops=2 * heads_kv * groups * tokens * keys_all * HD,
            bytes_accessed=2 * heads_kv * groups * tokens * (keys_all + HD),
            transcendentals=heads_kv * groups * tokens * keys_all,
        ),
        name="attention_weights",
    )(packed_len, queries, *key_blocks)


def weighted_values(weights, value_blocks):
    heads_kv, rows, keys_all = weights.shape
    tokens, columns = value_blocks[0].shape
    groups = rows // tokens

    def kernel(w_ref, *rest):
        value_refs, out_ref = rest[:-1], rest[-1]
        for g in range(heads_kv):
            cut = slice(g * HD, (g + 1) * HD)
            values = jnp.concatenate([ref[:, cut] for ref in value_refs], axis=0)
            mixed = jnp.dot(w_ref[g], values, preferred_element_type=jnp.float32)
            for j in range(groups):
                place = (g * groups + j) * HD
                out_ref[0, :, place : place + HD] = mixed[
                    j * tokens : (j + 1) * tokens, :
                ].astype(jnp.bfloat16)

    return pl.pallas_call(
        kernel,
        out_shape=jax.ShapeDtypeStruct((1, tokens, heads_kv * groups * HD), jnp.bfloat16),
        compiler_params=pltpu.CompilerParams(vmem_limit_bytes=24 * 2**20),
        cost_estimate=pl.CostEstimate(
            flops=2 * heads_kv * rows * keys_all * HD,
            bytes_accessed=2 * heads_kv * rows * keys_all,
            transcendentals=0,
        ),
        name="weighted_values",
    )(weights, *value_blocks)


def on_device(
    grad_parts,
    master_weight,
    moment_one,
    moment_two,
    queries,
    keys_in,
    hidden,
    segment_ids,
    packed_len,
):
    n_dp, n_replica = lax.axis_size("dp"), lax.axis_size("replica")
    tokens = queries.shape[1]
    rows, columns = master_weight.shape
    bits = bits_of(n_dp)
    orders = [bits, [bits[1], bits[0]] + bits[2:]]
    parts = len(orders)
    width = columns // parts
    state = (master_weight, moment_one, moment_two)

    flips = [halving(order) for order in orders]
    away = blocks_taken(grad_parts, [part[: n_dp // 2] for part in flips])
    came = [swapped(block, order[0] * n_replica) for block, order in zip(away, orders)]
    kept = list(blocks_taken(grad_parts, [part[n_dp // 2 :] for part in flips]))

    packed = packed_columns(hidden[0], rows, n_dp, n_replica)

    key_own = keys_and_numbers(keys_in, segment_ids)

    came[0], came[1], kept[0], kept[1], key_own, *packed = tied(
        came[0], came[1], kept[0], kept[1], key_own, *packed
    )
    streams = [[kept[part], came[part]] for part in range(parts)]
    token_blocks = [packed[0]] + [swapped(packed[m], m) for m in range(1, n_replica)]
    key_blocks = [passed_along(key_own, d) for d in (3, 2, 1)] + [key_own]
    state_here = staged(state)

    left = n_dp // 2
    for step in range(1, len(bits)):
        marks = [order[step] for order in orders]
        if marks[0] == marks[1]:
            both = swapped(first_half_sums(streams, left), marks[0] * n_replica)
            came = [both[part] for part in range(parts)]
        else:
            came = [
                swapped(first_half_sums([terms], left)[0], mark * n_replica)
                for terms, mark in zip(streams, marks)
            ]
        left = left // 2
        if step == 1:
            came[0], came[1], key_blocks[0], *state_here = tied(
                came[0], came[1], key_blocks[0], *state_here
            )
        if step == 2:
            came[0], came[1], token_blocks[2], key_blocks[1] = tied(
                came[0], came[1], token_blocks[2], key_blocks[1]
            )
        for part in range(parts):
            streams[part].append(came[part])

    fresh = fresh_rows(streams, state_here)
    grad_total = [
        sum(term[-1].astype(jnp.float32) for term in streams[part]) for part in range(parts)
    ]
    new_master, new_first, new_second = adam_update(
        jnp.concatenate(grad_total, axis=1), *state
    )
    labels = [[0] for _ in orders]
    for step in range(len(bits)):
        marks = [order[-1 - step] for order in orders]
        if marks[0] == marks[1]:
            came = swapped(fresh, marks[0] * n_replica)
            if step == 0:
                came, key_blocks[2], token_blocks[1] = tied(came, key_blocks[2], token_blocks[1])
                weights = attention_weights(packed_len, queries, key_blocks)
            joined = [one_below(fresh, came, part) for part in range(parts)]
            fresh = jnp.stack(joined) if step + 3 < len(bits) else None
        else:
            came = [swapped(joined[part], marks[part] * n_replica) for part in range(parts)]
            if step == len(bits) - 1:
                break
            came[0], came[1], *token_blocks = tied(came[0], came[1], *token_blocks)
            joined = [one_below(joined[part], came[part]) for part in range(parts)]
        labels = [own + [label ^ mark for label in own] for own, mark in zip(labels, marks)]
    last = [[label ^ mark for label in own] for own, mark in zip(labels, marks)]
    before = projected(token_blocks, list(zip(joined, labels)), rows, None)
    came[0], came[1], weights, before = tied(came[0], came[1], weights, before)
    partial, leaving = projected(token_blocks, list(zip(came, last)), rows, before)

    came = swapped(leaving, 1)
    partial = partial + came.astype(jnp.float32)
    for bit in bits_of(n_replica)[1:]:
        partial = partial.reshape(-1, 2, tokens, columns)
        came = swapped(partial[:, 1].astype(jnp.bfloat16), bit)
        partial = partial[:, 0] + came.astype(jnp.float32)
    value = partial[0].astype(jnp.bfloat16)
    value_blocks = [passed_along(value, d) for d in (3, 2, 1)] + [value]
    attended = weighted_values(weights, value_blocks)
    return (new_master, new_first, new_second, attended)


def solution(mesh):
    in_specs = (
        P("dp", "replica", None),
        P(("dp", "replica"), None),
        P(("dp", "replica"), None),
        P(("dp", "replica"), None),
        P("replica", "dp", None),
        P("replica", "dp", None),
        P("replica", "dp", None),
        P("replica", "dp"),
        P("replica"),
    )
    out_specs = (
        P(("dp", "replica"), None),
        P(("dp", "replica"), None),
        P(("dp", "replica"), None),
        P("replica", "dp", None),
    )
    return jax.shard_map(
        on_device, mesh=mesh, in_specs=in_specs, out_specs=out_specs, check_vma=False
    )
```

```python
import jax
import jax.numpy as jnp
from jax import lax
from jax.experimental import pallas as pl
from jax.experimental.pallas import tpu as pltpu
from jax.sharding import PartitionSpec as P

HD = 128
ALL = ("dp", "replica")
SMALL = 12 * 2**20

beta_one = 0.9
beta_two = 0.95
bias_one = 1.0 - 0.9**10
bias_two = 1.0 - 0.95**10
adam_eps = 1e-08
learn_rate = 0.002
weight_decay = 0.1


def bits_of(count):
    return [1 << j for j in range(count.bit_length() - 1)]


def swapped(block, mask):
    total = lax.axis_size("dp") * lax.axis_size("replica")
    return lax.ppermute(block, ALL, [(i, i ^ mask) for i in range(total)])


def preceding(block):
    n_dp = lax.axis_size("dp")
    two_before = lax.ppermute(block, "dp", [(i, i + 2) for i in range(n_dp - 2)])
    leaps = [(i, i + 1 + 2 * (i % 2)) for i in range(n_dp)]
    leapt = lax.ppermute(block, "dp", [leap for leap in leaps if leap[1] < n_dp])
    return [two_before, leapt, swapped(two_before, lax.axis_size("replica"))]


def in_order(two_before, leapt, relayed, own):
    odd = lax.axis_index("dp") % 2 == 1
    return [jnp.where(odd, relayed, leapt), two_before, jnp.where(odd, leapt, relayed), own]


def adam_update(grad_sum, master, moment_first, moment_second):
    first_new = beta_one * moment_first + (1.0 - beta_one) * grad_sum
    second_new = beta_two * moment_second + (1.0 - beta_two) * grad_sum * grad_sum
    step_dir = (
        first_new / bias_one / (jnp.sqrt(second_new / bias_two) + adam_eps) + weight_decay * master
    )
    master_new = master - learn_rate * step_dir
    return (master_new, first_new, second_new)


def tied(*values):
    return lax.optimization_barrier(values)


def halving(bits):
    if not bits:
        return [0]
    rest = halving(bits[1:])
    return [offset | bits[0] for offset in rest] + rest


def blocks_taken(terms, flips):
    _, rows, columns = terms.shape
    parts, blocks = len(flips), len(flips[0])
    width = columns // parts

    def kernel(terms_ref, *refs):
        out_refs, sems = refs[:parts], refs[parts]
        here = lax.axis_index("dp")
        copies = []
        for part in range(parts):
            for i, flip in enumerate(flips[part]):
                copies.append(
                    pltpu.make_async_copy(
                        terms_ref.at[here ^ flip, :, pl.ds(part * width, width)],
                        out_refs[part].at[i],
                        sems.at[part, i],
                    )
                )
        for copy in copies:
            copy.start()
        for copy in copies:
            copy.wait()

    return pl.pallas_call(
        kernel,
        in_specs=[pl.BlockSpec(memory_space=pltpu.HBM)],
        out_specs=[pl.BlockSpec(memory_space=pltpu.VMEM)] * parts,
        out_shape=[jax.ShapeDtypeStruct((blocks, rows, width), terms.dtype)] * parts,
        scratch_shapes=[pltpu.SemaphoreType.DMA((parts, blocks))],
        compiler_params=pltpu.CompilerParams(vmem_limit_bytes=SMALL),
        cost_estimate=pl.CostEstimate(
            flops=0, bytes_accessed=4 * blocks * rows * columns, transcendentals=0
        ),
        name="blocks_taken",
    )(terms)


def first_half_sums(streams, left):
    count = len(streams)
    sizes = [len(terms) for terms in streams]
    _, rows, width = streams[0][0].shape

    def kernel(*refs):
        out_ref = refs[-1]
        at = 0
        for i, size in enumerate(sizes):
            for j in range(left // 2):
                total = None
                for ref in refs[at : at + size]:
                    term = ref[ref.shape[0] - left + j].astype(jnp.float32)
                    total = term if total is None else total + term
                out_ref[i, j] = total.astype(jnp.bfloat16)
            at += size

    out = jax.ShapeDtypeStruct((count, left // 2, rows, width), jnp.bfloat16)
    return pl.pallas_call(
        kernel,
        out_shape=out,
        compiler_params=pltpu.CompilerParams(vmem_limit_bytes=SMALL),
        cost_estimate=pl.CostEstimate(
            flops=2 * sizes[0] * out.size, bytes_accessed=8 * out.size, transcendentals=0
        ),
        name="first_half_sums",
    )(*[term for terms in streams for term in terms])


def fresh_rows(streams, first_part, state):
    parts = len(streams)
    sizes = [len(terms) for terms in streams]
    _, rows, width = streams[0][0].shape

    def kernel(*refs):
        master_ref, first_ref, second_ref, out_ref = refs[-4:]
        at = 0
        for part, size in enumerate(sizes):
            grad = None
            for ref in refs[at : at + size]:
                term = ref[ref.shape[0] - 1].astype(jnp.float32)
                grad = term if grad is None else grad + term
            at += size
            cut = slice((first_part + part) * width, (first_part + part + 1) * width)
            updated = adam_update(grad, master_ref[:, cut], first_ref[:, cut], second_ref[:, cut])
            out_ref[part] = updated[0].astype(jnp.bfloat16)

    out = jax.ShapeDtypeStruct((parts, rows, width), jnp.bfloat16)
    return pl.pallas_call(
        kernel,
        out_shape=out,
        compiler_params=pltpu.CompilerParams(vmem_limit_bytes=SMALL),
        cost_estimate=pl.CostEstimate(
            flops=20 * out.size, bytes_accessed=20 * out.size, transcendentals=out.size
        ),
        name="fresh_rows",
    )(*[term for terms in streams for term in terms], *state)


def one_below(first, second, part=None):
    rows, width = first.shape[-2:]

    def kernel(first_ref, second_ref, out_ref):
        out_ref[:rows] = first_ref[...] if part is None else first_ref[part]
        out_ref[rows:] = second_ref[...] if part is None else second_ref[part]

    return pl.pallas_call(
        kernel,
        out_shape=jax.ShapeDtypeStruct((2 * rows, width), first.dtype),
        compiler_params=pltpu.CompilerParams(vmem_limit_bytes=SMALL),
        cost_estimate=pl.CostEstimate(
            flops=0, bytes_accessed=8 * rows * width, transcendentals=0
        ),
        name="one_below",
    )(first, second)


def staged(arrays):
    count = len(arrays)

    def kernel(*refs):
        for i in range(count):
            refs[count + i][...] = refs[i][...]

    rows, columns = arrays[0].shape
    return pl.pallas_call(
        kernel,
        grid=(2,),
        in_specs=[pl.BlockSpec((rows, columns // 2), lambda i: (0, i))] * count,
        out_specs=[pl.BlockSpec((rows, columns // 2), lambda i: (0, i))] * count,
        out_shape=[jax.ShapeDtypeStruct(x.shape, x.dtype) for x in arrays],
        compiler_params=pltpu.CompilerParams(vmem_limit_bytes=SMALL),
        cost_estimate=pl.CostEstimate(
            flops=0, bytes_accessed=8 * count * arrays[0].size, transcendentals=0
        ),
        name="staged",
    )(*arrays)


def packed_columns(hidden_rows, width, n_dp, n_replica):
    tokens = hidden_rows.shape[0]
    if width % HD:
        owner = lax.axis_index("dp") ^ jnp.arange(n_dp, dtype=jnp.int32)
        replica = lax.axis_index("replica") ^ jnp.arange(n_replica, dtype=jnp.int32)
        picks = owner[None, :] * n_replica + replica[:, None]
        cut = hidden_rows.reshape(tokens, -1, width)
        taken = jnp.take(cut, picks.reshape(-1), axis=1)
        taken = taken.reshape(tokens, n_replica, n_dp * width)
        return [taken[:, m] for m in range(n_replica)]

    def kernel(source_ref, *out_refs):
        dp, replica = lax.axis_index("dp"), lax.axis_index("replica")
        for m in range(n_replica):
            for o in range(n_dp):
                start = pl.multiple_of(((dp ^ o) * n_replica + (replica ^ m)) * width, width)
                out_refs[m][:, o * width : (o + 1) * width] = source_ref[:, pl.ds(start, width)]

    return pl.pallas_call(
        kernel,
        out_shape=[
            jax.ShapeDtypeStruct((tokens, n_dp * width), hidden_rows.dtype)
            for _ in range(n_replica)
        ],
        compiler_params=pltpu.CompilerParams(vmem_limit_bytes=16 * 2**20),
        cost_estimate=pl.CostEstimate(
            flops=0, bytes_accessed=4 * hidden_rows.size, transcendentals=0
        ),
        name="pack_hidden",
    )(hidden_rows)


def projected(token_blocks, pieces, width, before):
    count = len(token_blocks)
    parts = len(pieces)
    tokens = token_blocks[0].shape[0]
    depth, columns = pieces[0][0].shape

    def total_of(token_ref, weight_ref, places):
        total = None
        for i, place in enumerate(places):
            term = jnp.dot(
                token_ref[:, place * width : (place + 1) * width],
                weight_ref[i * width : (i + 1) * width, :],
                preferred_element_type=jnp.float32,
            )
            total = term if total is None else total + term
        return total

    def first_kernel(*refs):
        for m in range(count):
            for part in range(parts):
                total = total_of(refs[m], refs[count + part], pieces[part][1])
                refs[-1][m, :, part * columns : (part + 1) * columns] = total

    def last_kernel(*refs):
        kept_ref, away_ref = refs[-2], refs[-1]
        for m in range(count):
            for part in range(parts):
                cut = slice(part * columns, (part + 1) * columns)
                total = total_of(refs[m], refs[count + 1 + part], pieces[part][1])
                total = refs[count][m, :, cut] + total
                if m % 2:
                    away_ref[m // 2, :, cut] = total.astype(jnp.bfloat16)
                else:
                    kept_ref[m // 2, :, cut] = total

    cost = pl.CostEstimate(
        flops=2 * count * tokens * depth * columns * parts,
        bytes_accessed=2 * count * tokens * depth * parts,
        transcendentals=0,
    )
    params = pltpu.CompilerParams(vmem_limit_bytes=24 * 2**20)
    weights = [piece for piece, _ in pieces]
    if before is None:
        return pl.pallas_call(
            first_kernel,
            out_shape=jax.ShapeDtypeStruct((count, tokens, columns * parts), jnp.float32),
            compiler_params=params,
            cost_estimate=cost,
            name="projected_first",
        )(*token_blocks, *weights)
    return pl.pallas_call(
        last_kernel,
        out_shape=(
            jax.ShapeDtypeStruct((count // 2, tokens, columns * parts), jnp.float32),
            jax.ShapeDtypeStruct((count // 2, tokens, columns * parts), jnp.bfloat16),
        ),
        compiler_params=params,
        cost_estimate=cost,
        name="projected_last",
    )(*token_blocks, before, *weights)


def keys_and_numbers(keys_in, segment_ids):
    _, tokens, columns = keys_in.shape

    def kernel(key_ref, seg_ref, out_ref):
        out_ref[:tokens, :] = key_ref[0]
        numbers = seg_ref[...].astype(jnp.float32)
        numbers = jnp.concatenate([numbers] * (columns // tokens), axis=1)
        out_ref[tokens:, :] = jnp.broadcast_to(numbers, (16, columns)).astype(jnp.bfloat16)

    return pl.pallas_call(
        kernel,
        out_shape=jax.ShapeDtypeStruct((tokens + 16, columns), keys_in.dtype),
        compiler_params=pltpu.CompilerParams(vmem_limit_bytes=SMALL),
        name="keys_and_numbers",
    )(keys_in, segment_ids)


def attention_weights(packed_len, queries, key_blocks):
    tokens = queries.shape[1]
    heads_kv = key_blocks[0].shape[1] // HD
    groups = queries.shape[2] // (heads_kv * HD)
    spans = len(key_blocks)
    padded = key_blocks[0].shape[0]
    keys_all = spans * tokens

    def kernel(used_ref, q_ref, *rest):
        key_refs, out_ref = rest[:-1], rest[-1]
        here, used = lax.axis_index("dp"), used_ref[0]
        keys = jnp.concatenate(in_order(*[ref[0:tokens, :] for ref in key_refs]), axis=0)
        numbers = [ref[tokens : tokens + 16, :].astype(jnp.float32)[0:1, :] for ref in key_refs]
        seg_keys = jnp.concatenate(in_order(*numbers), axis=1)
        row = lax.broadcasted_iota(jnp.int32, (tokens, keys_all), 0)
        offset = lax.broadcasted_iota(jnp.int32, (tokens, keys_all), 1) - (spans - 1) * tokens
        seg_own = jnp.sum(jnp.where(offset == row, seg_keys, 0.0), axis=1, keepdims=True)
        allowed = (seg_own == seg_keys) & (offset <= row) & (offset + here * tokens >= 0)
        live = (here * tokens + lax.broadcasted_iota(jnp.int32, (tokens, 1), 0)) < used
        for j in range(groups):
            scores = lax.dot_general(
                q_ref[0, :, j * HD : (j + 1) * HD],
                keys,
                (((1,), (1,)), ((), ())),
                preferred_element_type=jnp.float32,
            ) * HD ** (-0.5)
            scores = jnp.where(allowed, scores, -1e30)
            weights = jnp.exp(scores - jnp.max(scores, axis=-1, keepdims=True))
            totals = jnp.sum(weights, axis=-1, keepdims=True)
            scale = jnp.where(live, 1.0 / totals, 0.0)
            out_ref[0, j * tokens : (j + 1) * tokens, :] = (weights * scale).astype(jnp.bfloat16)

    key_spec = pl.BlockSpec((padded, HD), lambda g: (0, g))
    return pl.pallas_call(
        kernel,
        grid=(heads_kv,),
        out_shape=jax.ShapeDtypeStruct((heads_kv, groups * tokens, keys_all), jnp.bfloat16),
        in_specs=[
            pl.BlockSpec(memory_space=pltpu.SMEM),
            pl.BlockSpec((1, tokens, groups * HD), lambda g: (0, 0, g)),
        ]
        + [key_spec] * spans,
        out_specs=pl.BlockSpec((1, groups * tokens, keys_all), lambda g: (g, 0, 0)),
        compiler_params=pltpu.CompilerParams(vmem_limit_bytes=16 * 2**20),
        cost_estimate=pl.CostEstimate(
            flops=2 * heads_kv * groups * tokens * keys_all * HD,
            bytes_accessed=2 * heads_kv * groups * tokens * (keys_all + HD),
            transcendentals=heads_kv * groups * tokens * keys_all,
        ),
        name="attention_weights",
    )(packed_len, queries, *key_blocks)


def weighted_values(weights, value_blocks):
    heads_kv, rows, keys_all = weights.shape
    tokens, columns = value_blocks[0].shape
    groups = rows // tokens

    def kernel(w_ref, *rest):
        value_refs, out_ref = rest[:-1], rest[-1]
        for g in range(heads_kv):
            cut = slice(g * HD, (g + 1) * HD)
            values = jnp.concatenate(in_order(*[ref[:, cut] for ref in value_refs]), axis=0)
            mixed = jnp.dot(w_ref[g], values, preferred_element_type=jnp.float32)
            for j in range(groups):
                place = (g * groups + j) * HD
                out_ref[0, :, place : place + HD] = mixed[
                    j * tokens : (j + 1) * tokens, :
                ].astype(jnp.bfloat16)

    return pl.pallas_call(
        kernel,
        out_shape=jax.ShapeDtypeStruct((1, tokens, heads_kv * groups * HD), jnp.bfloat16),
        compiler_params=pltpu.CompilerParams(vmem_limit_bytes=24 * 2**20),
        cost_estimate=pl.CostEstimate(
            flops=2 * heads_kv * rows * keys_all * HD,
            bytes_accessed=2 * heads_kv * rows * keys_all,
            transcendentals=0,
        ),
        name="weighted_values",
    )(weights, *value_blocks)


def on_device(
    grad_parts,
    master_weight,
    moment_one,
    moment_two,
    queries,
    keys_in,
    hidden,
    segment_ids,
    packed_len,
):
    n_dp, n_replica = lax.axis_size("dp"), lax.axis_size("replica")
    tokens = queries.shape[1]
    rows, columns = master_weight.shape
    bits = bits_of(n_dp)
    orders = [bits, [bits[1], bits[0]] + bits[2:]]
    parts = len(orders)
    width = columns // parts
    state = (master_weight, moment_one, moment_two)

    flips = [halving(order) for order in orders]
    away = blocks_taken(grad_parts, [part[: n_dp // 2] for part in flips])
    came = [swapped(block, order[0] * n_replica) for block, order in zip(away, orders)]
    kept = list(blocks_taken(grad_parts, [part[n_dp // 2 :] for part in flips]))

    packed = packed_columns(hidden[0], rows, n_dp, n_replica)

    key_own = keys_and_numbers(keys_in, segment_ids)

    came[0], came[1], kept[0], kept[1], key_own, *packed = tied(
        came[0], came[1], kept[0], kept[1], key_own, *packed
    )
    key_blocks = preceding(key_own) + [key_own]
    streams = [[kept[part], came[part]] for part in range(parts)]
    token_blocks = [packed[0]] + [swapped(packed[m], m) for m in range(1, n_replica)]
    state_here = staged(state)

    left = n_dp // 2
    for step in range(1, len(bits)):
        for part in range(parts):
            mark = orders[part][step] * n_replica
            came[part] = swapped(first_half_sums([streams[part]], left)[0], mark)
        left = left // 2
        if step == 1:
            came[0], *state_here = tied(came[0], *state_here)
        if step == 2:
            came[0], token_blocks[2] = tied(came[0], token_blocks[2])
        for part in range(parts):
            streams[part].append(came[part])

    fresh = [fresh_rows([terms], part, state_here)[0] for part, terms in enumerate(streams)]
    grad_total = [
        sum(term[-1].astype(jnp.float32) for term in streams[part]) for part in range(parts)
    ]
    new_master, new_first, new_second = adam_update(jnp.concatenate(grad_total, axis=1), *state)
    labels = [[0] for _ in orders]
    for step in range(len(bits)):
        marks = [order[-1 - step] for order in orders]
        came = [swapped(fresh[part], marks[part] * n_replica) for part in range(parts)]
        if step == 0:
            came[0], token_blocks[1] = tied(came[0], token_blocks[1])
        if step == 1:
            came[0], *token_blocks = tied(came[0], *token_blocks)
            came[1], *key_blocks = tied(came[1], *key_blocks)
        if step < len(bits) - 1:
            fresh = [one_below(fresh[part], came[part]) for part in range(parts)]
            labels = [own + [label ^ mark for label in own] for own, mark in zip(labels, marks)]
    weights = attention_weights(packed_len, queries, key_blocks)
    joined = fresh
    last = [[label ^ mark for label in own] for own, mark in zip(labels, marks)]
    before = projected(token_blocks, list(zip(joined, labels)), rows, None)
    came[0], came[1], weights, before = tied(came[0], came[1], weights, before)
    partial, leaving = projected(token_blocks, list(zip(came, last)), rows, before)

    came = swapped(leaving, 1)
    partial = partial + came.astype(jnp.float32)
    for bit in bits_of(n_replica)[1:]:
        partial = partial.reshape(-1, 2, tokens, columns)
        leaving = partial[:, 1].astype(jnp.bfloat16)
        came = swapped(leaving, bit)
        partial = partial[:, 0] + came.astype(jnp.float32)
    value = partial[0].astype(jnp.bfloat16)
    value_blocks = preceding(value) + [value]
    attended = weighted_values(weights, value_blocks)
    return (new_master, new_first, new_second, attended)


def solution(mesh):
    in_specs = (
        P("dp", "replica", None),
        P(("dp", "replica"), None),
        P(("dp", "replica"), None),
        P(("dp", "replica"), None),
        P("replica", "dp", None),
        P("replica", "dp", None),
        P("replica", "dp", None),
        P("replica", "dp"),
        P("replica"),
    )
    out_specs = (
        P(("dp", "replica"), None),
        P(("dp", "replica"), None),
        P(("dp", "replica"), None),
        P("replica", "dp", None),
    )
    return jax.shard_map(
        on_device, mesh=mesh, in_specs=in_specs, out_specs=out_specs, check_vma=False
    )
```

```python
import jax
import jax.numpy as jnp
from jax import lax
from jax.experimental import pallas as pl
from jax.experimental.pallas import tpu as pltpu
from jax.sharding import PartitionSpec as P

HD = 128
ALL = ("dp", "replica")
SMALL = 12 * 2**20

beta_one = 0.9
beta_two = 0.95
bias_one = 1.0 - 0.9**10
bias_two = 1.0 - 0.95**10
adam_eps = 1e-08
learn_rate = 0.002
weight_decay = 0.1


def bits_of(count):
    return [1 << j for j in range(count.bit_length() - 1)]


def swapped(block, mask):
    total = lax.axis_size("dp") * lax.axis_size("replica")
    return lax.ppermute(block, ALL, [(i, i ^ mask) for i in range(total)])


def preceding(block):
    n_dp = lax.axis_size("dp")
    two_before = lax.ppermute(block, "dp", [(i, (i + 2) % n_dp) for i in range(n_dp)])
    leaps = [(i, i + 1 + 2 * (i % 2)) for i in range(n_dp)]
    leapt = lax.ppermute(block, "dp", [leap for leap in leaps if leap[1] < n_dp])
    return [two_before, leapt, swapped(two_before, lax.axis_size("replica"))]


def in_order(two_before, leapt, relayed, own):
    odd = lax.axis_index("dp") % 2 == 1
    return [jnp.where(odd, relayed, leapt), two_before, jnp.where(odd, leapt, relayed), own]


def adam_update(grad_sum, master, moment_first, moment_second):
    first_new = beta_one * moment_first + (1.0 - beta_one) * grad_sum
    second_new = beta_two * moment_second + (1.0 - beta_two) * grad_sum * grad_sum
    step_dir = (
        first_new / bias_one / (jnp.sqrt(second_new / bias_two) + adam_eps) + weight_decay * master
    )
    master_new = master - learn_rate * step_dir
    return (master_new, first_new, second_new)


def tied(*values):
    return lax.optimization_barrier(values)


def halving(bits):
    if not bits:
        return [0]
    rest = halving(bits[1:])
    return [offset | bits[0] for offset in rest] + rest


def blocks_taken(terms, flips):
    _, rows, columns = terms.shape
    parts, blocks = len(flips), len(flips[0])
    width = columns // parts

    def kernel(terms_ref, *refs):
        out_refs, sems = refs[:parts], refs[parts]
        here = lax.axis_index("dp")
        copies = []
        for part in range(parts):
            for i, flip in enumerate(flips[part]):
                copies.append(
                    pltpu.make_async_copy(
                        terms_ref.at[here ^ flip, :, pl.ds(part * width, width)],
                        out_refs[part].at[i],
                        sems.at[part, i],
                    )
                )
        for copy in copies:
            copy.start()
        for copy in copies:
            copy.wait()

    return pl.pallas_call(
        kernel,
        in_specs=[pl.BlockSpec(memory_space=pltpu.HBM)],
        out_specs=[pl.BlockSpec(memory_space=pltpu.VMEM)] * parts,
        out_shape=[jax.ShapeDtypeStruct((blocks, rows, width), terms.dtype)] * parts,
        scratch_shapes=[pltpu.SemaphoreType.DMA((parts, blocks))],
        compiler_params=pltpu.CompilerParams(vmem_limit_bytes=SMALL),
        cost_estimate=pl.CostEstimate(
            flops=0, bytes_accessed=4 * blocks * rows * columns, transcendentals=0
        ),
        name="blocks_taken",
    )(terms)


def first_half_sums(streams, left):
    count = len(streams)
    sizes = [len(terms) for terms in streams]
    _, rows, width = streams[0][0].shape

    def kernel(*refs):
        out_ref = refs[-1]
        at = 0
        for i, size in enumerate(sizes):
            for j in range(left // 2):
                total = None
                for ref in refs[at : at + size]:
                    term = ref[ref.shape[0] - left + j].astype(jnp.float32)
                    total = term if total is None else total + term
                out_ref[i, j] = total.astype(jnp.bfloat16)
            at += size

    out = jax.ShapeDtypeStruct((count, left // 2, rows, width), jnp.bfloat16)
    return pl.pallas_call(
        kernel,
        out_shape=out,
        compiler_params=pltpu.CompilerParams(vmem_limit_bytes=SMALL),
        cost_estimate=pl.CostEstimate(
            flops=2 * sizes[0] * out.size, bytes_accessed=8 * out.size, transcendentals=0
        ),
        name="first_half_sums",
    )(*[term for terms in streams for term in terms])


def fresh_rows(streams, first_part, state):
    parts = len(streams)
    sizes = [len(terms) for terms in streams]
    _, rows, width = streams[0][0].shape

    def kernel(*refs):
        master_ref, first_ref, second_ref, out_ref = refs[-4:]
        at = 0
        for part, size in enumerate(sizes):
            grad = None
            for ref in refs[at : at + size]:
                term = ref[ref.shape[0] - 1].astype(jnp.float32)
                grad = term if grad is None else grad + term
            at += size
            cut = slice((first_part + part) * width, (first_part + part + 1) * width)
            updated = adam_update(grad, master_ref[:, cut], first_ref[:, cut], second_ref[:, cut])
            out_ref[part] = updated[0].astype(jnp.bfloat16)

    out = jax.ShapeDtypeStruct((parts, rows, width), jnp.bfloat16)
    return pl.pallas_call(
        kernel,
        out_shape=out,
        compiler_params=pltpu.CompilerParams(vmem_limit_bytes=SMALL),
        cost_estimate=pl.CostEstimate(
            flops=20 * out.size, bytes_accessed=20 * out.size, transcendentals=out.size
        ),
        name="fresh_rows",
    )(*[term for terms in streams for term in terms], *state)


def one_below(first, second, part=None):
    rows, width = first.shape[-2:]

    def kernel(first_ref, second_ref, out_ref):
        out_ref[:rows] = first_ref[...] if part is None else first_ref[part]
        out_ref[rows:] = second_ref[...] if part is None else second_ref[part]

    return pl.pallas_call(
        kernel,
        out_shape=jax.ShapeDtypeStruct((2 * rows, width), first.dtype),
        compiler_params=pltpu.CompilerParams(vmem_limit_bytes=SMALL),
        cost_estimate=pl.CostEstimate(
            flops=0, bytes_accessed=8 * rows * width, transcendentals=0
        ),
        name="one_below",
    )(first, second)


def staged(arrays):
    count = len(arrays)

    def kernel(*refs):
        for i in range(count):
            refs[count + i][...] = refs[i][...]

    rows, columns = arrays[0].shape
    return pl.pallas_call(
        kernel,
        grid=(2,),
        in_specs=[pl.BlockSpec((rows, columns // 2), lambda i: (0, i))] * count,
        out_specs=[pl.BlockSpec((rows, columns // 2), lambda i: (0, i))] * count,
        out_shape=[jax.ShapeDtypeStruct(x.shape, x.dtype) for x in arrays],
        compiler_params=pltpu.CompilerParams(vmem_limit_bytes=SMALL),
        cost_estimate=pl.CostEstimate(
            flops=0, bytes_accessed=8 * count * arrays[0].size, transcendentals=0
        ),
        name="staged",
    )(*arrays)


def packed_columns(hidden_rows, width, n_dp, n_replica):
    tokens = hidden_rows.shape[0]
    if width % HD:
        owner = lax.axis_index("dp") ^ jnp.arange(n_dp, dtype=jnp.int32)
        replica = lax.axis_index("replica") ^ jnp.arange(n_replica, dtype=jnp.int32)
        picks = owner[None, :] * n_replica + replica[:, None]
        cut = hidden_rows.reshape(tokens, -1, width)
        taken = jnp.take(cut, picks.reshape(-1), axis=1)
        taken = taken.reshape(tokens, n_replica, n_dp * width)
        return [taken[:, m] for m in range(n_replica)]

    def kernel(source_ref, *out_refs):
        dp, replica = lax.axis_index("dp"), lax.axis_index("replica")
        for m in range(n_replica):
            for o in range(n_dp):
                start = pl.multiple_of(((dp ^ o) * n_replica + (replica ^ m)) * width, width)
                out_refs[m][:, o * width : (o + 1) * width] = source_ref[:, pl.ds(start, width)]

    return pl.pallas_call(
        kernel,
        out_shape=[
            jax.ShapeDtypeStruct((tokens, n_dp * width), hidden_rows.dtype)
            for _ in range(n_replica)
        ],
        compiler_params=pltpu.CompilerParams(vmem_limit_bytes=16 * 2**20),
        cost_estimate=pl.CostEstimate(
            flops=0, bytes_accessed=4 * hidden_rows.size, transcendentals=0
        ),
        name="pack_hidden",
    )(hidden_rows)


def projected(token_blocks, pieces, width, before):
    count = len(token_blocks)
    parts = len(pieces)
    tokens = token_blocks[0].shape[0]
    depth, columns = pieces[0][0].shape

    def total_of(token_ref, weight_ref, places):
        total = None
        for i, place in enumerate(places):
            term = jnp.dot(
                token_ref[:, place * width : (place + 1) * width],
                weight_ref[i * width : (i + 1) * width, :],
                preferred_element_type=jnp.float32,
            )
            total = term if total is None else total + term
        return total

    def first_kernel(*refs):
        for m in range(count):
            for part in range(parts):
                total = total_of(refs[m], refs[count + part], pieces[part][1])
                refs[-1][m, :, part * columns : (part + 1) * columns] = total

    def last_kernel(*refs):
        kept_ref, away_ref = refs[-2], refs[-1]
        for m in range(count):
            for part in range(parts):
                cut = slice(part * columns, (part + 1) * columns)
                total = total_of(refs[m], refs[count + 1 + part], pieces[part][1])
                total = refs[count][m, :, cut] + total
                if m % 2:
                    away_ref[m // 2, :, cut] = total.astype(jnp.bfloat16)
                else:
                    kept_ref[m // 2, :, cut] = total

    cost = pl.CostEstimate(
        flops=2 * count * tokens * depth * columns * parts,
        bytes_accessed=2 * count * tokens * depth * parts,
        transcendentals=0,
    )
    params = pltpu.CompilerParams(vmem_limit_bytes=24 * 2**20)
    weights = [piece for piece, _ in pieces]
    if before is None:
        return pl.pallas_call(
            first_kernel,
            out_shape=jax.ShapeDtypeStruct((count, tokens, columns * parts), jnp.float32),
            compiler_params=params,
            cost_estimate=cost,
            name="projected_first",
        )(*token_blocks, *weights)
    return pl.pallas_call(
        last_kernel,
        out_shape=(
            jax.ShapeDtypeStruct((count // 2, tokens, columns * parts), jnp.float32),
            jax.ShapeDtypeStruct((count // 2, tokens, columns * parts), jnp.bfloat16),
        ),
        compiler_params=params,
        cost_estimate=cost,
        name="projected_last",
    )(*token_blocks, before, *weights)


def keys_and_numbers(keys_in, segment_ids):
    _, tokens, columns = keys_in.shape

    def kernel(key_ref, seg_ref, out_ref):
        out_ref[:tokens, :] = key_ref[0]
        numbers = seg_ref[...].astype(jnp.float32)
        numbers = jnp.concatenate([numbers] * (columns // tokens), axis=1)
        out_ref[tokens:, :] = jnp.broadcast_to(numbers, (16, columns)).astype(jnp.bfloat16)

    return pl.pallas_call(
        kernel,
        out_shape=jax.ShapeDtypeStruct((tokens + 16, columns), keys_in.dtype),
        compiler_params=pltpu.CompilerParams(vmem_limit_bytes=SMALL),
        name="keys_and_numbers",
    )(keys_in, segment_ids)


def attention_weights(packed_len, queries, key_blocks):
    tokens = queries.shape[1]
    heads_kv = key_blocks[0].shape[1] // HD
    groups = queries.shape[2] // (heads_kv * HD)
    spans = len(key_blocks)
    padded = key_blocks[0].shape[0]
    keys_all = spans * tokens

    def kernel(used_ref, q_ref, *rest):
        key_refs, out_ref = rest[:-1], rest[-1]
        here, used = lax.axis_index("dp"), used_ref[0]
        keys = jnp.concatenate(in_order(*[ref[0:tokens, :] for ref in key_refs]), axis=0)
        numbers = [ref[tokens : tokens + 16, :].astype(jnp.float32)[0:1, :] for ref in key_refs]
        seg_keys = jnp.concatenate(in_order(*numbers), axis=1)
        row = lax.broadcasted_iota(jnp.int32, (tokens, keys_all), 0)
        offset = lax.broadcasted_iota(jnp.int32, (tokens, keys_all), 1) - (spans - 1) * tokens
        seg_own = jnp.sum(jnp.where(offset == row, seg_keys, 0.0), axis=1, keepdims=True)
        allowed = (seg_own == seg_keys) & (offset <= row) & (offset + here * tokens >= 0)
        live = (here * tokens + lax.broadcasted_iota(jnp.int32, (tokens, 1), 0)) < used
        for j in range(groups):
            scores = lax.dot_general(
                q_ref[0, :, j * HD : (j + 1) * HD],
                keys,
                (((1,), (1,)), ((), ())),
                preferred_element_type=jnp.float32,
            ) * HD ** (-0.5)
            scores = jnp.where(allowed, scores, -1e30)
            weights = jnp.exp(scores - jnp.max(scores, axis=-1, keepdims=True))
            totals = jnp.sum(weights, axis=-1, keepdims=True)
            scale = jnp.where(live, 1.0 / totals, 0.0)
            out_ref[0, j * tokens : (j + 1) * tokens, :] = (weights * scale).astype(jnp.bfloat16)

    key_spec = pl.BlockSpec((padded, HD), lambda g: (0, g))
    return pl.pallas_call(
        kernel,
        grid=(heads_kv,),
        out_shape=jax.ShapeDtypeStruct((heads_kv, groups * tokens, keys_all), jnp.bfloat16),
        in_specs=[
            pl.BlockSpec(memory_space=pltpu.SMEM),
            pl.BlockSpec((1, tokens, groups * HD), lambda g: (0, 0, g)),
        ]
        + [key_spec] * spans,
        out_specs=pl.BlockSpec((1, groups * tokens, keys_all), lambda g: (g, 0, 0)),
        compiler_params=pltpu.CompilerParams(vmem_limit_bytes=16 * 2**20),
        cost_estimate=pl.CostEstimate(
            flops=2 * heads_kv * groups * tokens * keys_all * HD,
            bytes_accessed=2 * heads_kv * groups * tokens * (keys_all + HD),
            transcendentals=heads_kv * groups * tokens * keys_all,
        ),
        name="attention_weights",
    )(packed_len, queries, *key_blocks)


def weighted_values_early(weights, two_before, own):
    heads_kv, rows, _ = weights.shape
    tokens = own.shape[0]

    def kernel(w_ref, before_ref, own_ref, out_ref):
        for g in range(heads_kv):
            cut = slice(g * HD, (g + 1) * HD)
            picked = jnp.concatenate(
                [w_ref[g, :, tokens : 2 * tokens], w_ref[g, :, 3 * tokens : 4 * tokens]], axis=1
            )
            values = jnp.concatenate([before_ref[:, cut], own_ref[:, cut]], axis=0)
            out_ref[g] = jnp.dot(picked, values, preferred_element_type=jnp.float32)

    return pl.pallas_call(
        kernel,
        out_shape=jax.ShapeDtypeStruct((heads_kv, rows, HD), jnp.float32),
        compiler_params=pltpu.CompilerParams(vmem_limit_bytes=16 * 2**20),
        cost_estimate=pl.CostEstimate(
            flops=4 * heads_kv * rows * tokens * HD,
            bytes_accessed=4 * heads_kv * rows * tokens,
            transcendentals=0,
        ),
        name="weighted_values_early",
    )(weights, two_before, own)


def weighted_values(weights, early, leapt, relayed):
    heads_kv, rows, _ = weights.shape
    tokens = leapt.shape[0]
    groups = rows // tokens
    span = groups * HD

    def kernel(w_ref, early_ref, leapt_ref, relayed_ref, out_ref, mixed_ref, sems):
        copies = []
        for g in range(heads_kv):
            cut = slice(g * HD, (g + 1) * HD)
            picked = jnp.concatenate(
                [w_ref[g, :, 0:tokens], w_ref[g, :, 2 * tokens : 3 * tokens]], axis=1
            )
            oldest, _, last, _ = in_order(None, leapt_ref[:, cut], relayed_ref[:, cut], None)
            values = jnp.concatenate([oldest, last], axis=0)
            mixed = early_ref[g] + jnp.dot(picked, values, preferred_element_type=jnp.float32)
            for j in range(groups):
                mixed_ref[:, g * span + j * HD : g * span + (j + 1) * HD] = mixed[
                    j * tokens : (j + 1) * tokens, :
                ].astype(jnp.bfloat16)
            here = pl.ds(g * span, span)
            copies.append(
                pltpu.make_async_copy(mixed_ref.at[:, here], out_ref.at[0, :, here], sems.at[g])
            )
            copies[-1].start()
        for copy in copies:
            copy.wait()

    return pl.pallas_call(
        kernel,
        out_shape=jax.ShapeDtypeStruct((1, tokens, heads_kv * span), jnp.bfloat16),
        in_specs=[pl.BlockSpec(memory_space=pltpu.VMEM)] * 4,
        out_specs=pl.BlockSpec(memory_space=pltpu.HBM),
        scratch_shapes=[
            pltpu.VMEM((tokens, heads_kv * span), jnp.bfloat16),
            pltpu.SemaphoreType.DMA((heads_kv,)),
        ],
        compiler_params=pltpu.CompilerParams(vmem_limit_bytes=24 * 2**20),
        cost_estimate=pl.CostEstimate(
            flops=4 * heads_kv * rows * tokens * HD,
            bytes_accessed=4 * heads_kv * rows * tokens,
            transcendentals=0,
        ),
        name="weighted_values",
    )(weights, early, leapt, relayed)


def on_device(
    grad_parts,
    master_weight,
    moment_one,
    moment_two,
    queries,
    keys_in,
    hidden,
    segment_ids,
    packed_len,
):
    n_dp, n_replica = lax.axis_size("dp"), lax.axis_size("replica")
    tokens = queries.shape[1]
    rows, columns = master_weight.shape
    bits = bits_of(n_dp)
    orders = [bits, [bits[1], bits[0]] + bits[2:]]
    parts = len(orders)
    width = columns // parts
    state = (master_weight, moment_one, moment_two)

    flips = [halving(order) for order in orders]
    away = blocks_taken(grad_parts, [part[: n_dp // 2] for part in flips])
    came = [swapped(block, order[0] * n_replica) for block, order in zip(away, orders)]
    kept = list(blocks_taken(grad_parts, [part[n_dp // 2 :] for part in flips]))

    packed = packed_columns(hidden[0], rows, n_dp, n_replica)

    key_own = keys_and_numbers(keys_in, segment_ids)

    came[0], came[1], kept[0], kept[1], key_own, *packed = tied(
        came[0], came[1], kept[0], kept[1], key_own, *packed
    )
    key_blocks = preceding(key_own) + [key_own]
    streams = [[kept[part], came[part]] for part in range(parts)]
    token_blocks = [packed[0]] + [swapped(packed[m], m) for m in range(1, n_replica)]
    state_here = staged(state)

    left = n_dp // 2
    for step in range(1, len(bits)):
        for part in range(parts):
            mark = orders[part][step] * n_replica
            came[part] = swapped(first_half_sums([streams[part]], left)[0], mark)
        left = left // 2
        if step == 1:
            came[0], *state_here = tied(came[0], *state_here)
        if step == 2:
            came[0], token_blocks[2] = tied(came[0], token_blocks[2])
        for part in range(parts):
            streams[part].append(came[part])

    fresh = [fresh_rows([terms], part, state_here)[0] for part, terms in enumerate(streams)]
    grad_total = [
        sum(term[-1].astype(jnp.float32) for term in streams[part]) for part in range(parts)
    ]
    new_master, new_first, new_second = adam_update(jnp.concatenate(grad_total, axis=1), *state)
    labels = [[0] for _ in orders]
    for step in range(len(bits)):
        marks = [order[-1 - step] for order in orders]
        came = [swapped(fresh[part], marks[part] * n_replica) for part in range(parts)]
        if step == 0:
            came[0], token_blocks[1] = tied(came[0], token_blocks[1])
        if step == 1:
            came[0], *token_blocks = tied(came[0], *token_blocks)
            came[0], *key_blocks = tied(came[0], *key_blocks)
        if step < len(bits) - 1:
            fresh = [one_below(fresh[part], came[part]) for part in range(parts)]
            labels = [own + [label ^ mark for label in own] for own, mark in zip(labels, marks)]
    weights = attention_weights(packed_len, queries, key_blocks)
    joined = fresh
    last = [[label ^ mark for label in own] for own, mark in zip(labels, marks)]
    before = projected(token_blocks, list(zip(joined, labels)), rows, None)
    came[0], came[1], weights, before = tied(came[0], came[1], weights, before)
    partial, leaving = projected(token_blocks, list(zip(came, last)), rows, before)

    came = swapped(leaving, 1)
    partial = partial + came.astype(jnp.float32)
    for bit in bits_of(n_replica)[1:]:
        partial = partial.reshape(-1, 2, tokens, columns)
        leaving = partial[:, 1].astype(jnp.bfloat16)
        came = swapped(leaving, bit)
        partial = partial[:, 0] + came.astype(jnp.float32)
    value = partial[0].astype(jnp.bfloat16)
    two_before, leapt, relayed = preceding(value)
    early = weighted_values_early(weights, two_before, value)
    attended = weighted_values(weights, early, leapt, relayed)
    return (new_master, new_first, new_second, attended)


def solution(mesh):
    in_specs = (
        P("dp", "replica", None),
        P(("dp", "replica"), None),
        P(("dp", "replica"), None),
        P(("dp", "replica"), None),
        P("replica", "dp", None),
        P("replica", "dp", None),
        P("replica", "dp", None),
        P("replica", "dp"),
        P("replica"),
    )
    out_specs = (
        P(("dp", "replica"), None),
        P(("dp", "replica"), None),
        P(("dp", "replica"), None),
        P("replica", "dp", None),
    )
    return jax.shard_map(
        on_device, mesh=mesh, in_specs=in_specs, out_specs=out_specs, check_vma=False
    )
```

```python
import jax
import jax.numpy as jnp
from jax import lax
from jax.experimental import pallas as pl
from jax.experimental.pallas import tpu as pltpu
from jax.sharding import PartitionSpec as P

HD = 128
ALL = ("dp", "replica")
SMALL = 12 * 2**20

beta_one = 0.9
beta_two = 0.95
bias_one = 1.0 - 0.9**10
bias_two = 1.0 - 0.95**10
adam_eps = 1e-08
learn_rate = 0.002
weight_decay = 0.1


def bits_of(count):
    return [1 << j for j in range(count.bit_length() - 1)]


def swapped(block, mask):
    total = lax.axis_size("dp") * lax.axis_size("replica")
    return lax.ppermute(block, ALL, [(i, i ^ mask) for i in range(total)])


def preceding(block, wraps):
    n_dp = lax.axis_size("dp")
    reach = n_dp if wraps else n_dp - 2
    two_before = lax.ppermute(block, "dp", [(i, (i + 2) % n_dp) for i in range(reach)])
    leaps = [(i, i + 1 + 2 * (i % 2)) for i in range(n_dp)]
    leapt = lax.ppermute(block, "dp", [leap for leap in leaps if leap[1] < n_dp])
    return [two_before, leapt, swapped(two_before, lax.axis_size("replica"))]


def in_order(two_before, leapt, relayed, own):
    odd = lax.axis_index("dp") % 2 == 1
    return [jnp.where(odd, relayed, leapt), two_before, jnp.where(odd, leapt, relayed), own]


def adam_update(grad_sum, master, moment_first, moment_second):
    first_new = beta_one * moment_first + (1.0 - beta_one) * grad_sum
    second_new = beta_two * moment_second + (1.0 - beta_two) * grad_sum * grad_sum
    step_dir = (
        first_new / bias_one / (jnp.sqrt(second_new / bias_two) + adam_eps) + weight_decay * master
    )
    master_new = master - learn_rate * step_dir
    return (master_new, first_new, second_new)


def tied(*values):
    return lax.optimization_barrier(values)


def halving(bits):
    if not bits:
        return [0]
    rest = halving(bits[1:])
    return [offset | bits[0] for offset in rest] + rest


def blocks_taken(terms, flips, cuts):
    _, rows, columns = terms.shape
    parts, blocks = len(flips), len(flips[0])

    def kernel(terms_ref, *refs):
        out_refs, sems = refs[:parts], refs[parts]
        here = lax.axis_index("dp")
        copies = []
        for part in range(parts):
            for i, flip in enumerate(flips[part]):
                copies.append(
                    pltpu.make_async_copy(
                        terms_ref.at[here ^ flip, :, pl.ds(*cuts[part])],
                        out_refs[part].at[i],
                        sems.at[part, i],
                    )
                )
        for copy in copies:
            copy.start()
        for copy in copies:
            copy.wait()

    return pl.pallas_call(
        kernel,
        in_specs=[pl.BlockSpec(memory_space=pltpu.HBM)],
        out_specs=[pl.BlockSpec(memory_space=pltpu.VMEM)] * parts,
        out_shape=[
            jax.ShapeDtypeStruct((blocks, rows, width), terms.dtype) for _, width in cuts
        ],
        scratch_shapes=[pltpu.SemaphoreType.DMA((parts, blocks))],
        compiler_params=pltpu.CompilerParams(vmem_limit_bytes=SMALL),
        cost_estimate=pl.CostEstimate(
            flops=0, bytes_accessed=4 * blocks * rows * columns, transcendentals=0
        ),
        name="blocks_taken",
    )(terms)


def first_half_sums(streams, left):
    count = len(streams)
    sizes = [len(terms) for terms in streams]
    _, rows, width = streams[0][0].shape

    def kernel(*refs):
        out_ref = refs[-1]
        at = 0
        for i, size in enumerate(sizes):
            for j in range(left // 2):
                total = None
                for ref in refs[at : at + size]:
                    term = ref[ref.shape[0] - left + j].astype(jnp.float32)
                    total = term if total is None else total + term
                out_ref[i, j] = total.astype(jnp.bfloat16)
            at += size

    out = jax.ShapeDtypeStruct((count, left // 2, rows, width), jnp.bfloat16)
    return pl.pallas_call(
        kernel,
        out_shape=out,
        compiler_params=pltpu.CompilerParams(vmem_limit_bytes=SMALL),
        cost_estimate=pl.CostEstimate(
            flops=2 * sizes[0] * out.size, bytes_accessed=8 * out.size, transcendentals=0
        ),
        name="first_half_sums",
    )(*[term for terms in streams for term in terms])


def fresh_rows(terms, start, state):
    _, rows, width = terms[0].shape

    def kernel(*refs):
        master_ref, first_ref, second_ref, out_ref = refs[-4:]
        grad = None
        for ref in refs[:-4]:
            term = ref[ref.shape[0] - 1].astype(jnp.float32)
            grad = term if grad is None else grad + term
        cut = slice(start, start + width)
        updated = adam_update(grad, master_ref[:, cut], first_ref[:, cut], second_ref[:, cut])
        out_ref[...] = updated[0].astype(jnp.bfloat16)

    out = jax.ShapeDtypeStruct((rows, width), jnp.bfloat16)
    return pl.pallas_call(
        kernel,
        out_shape=out,
        compiler_params=pltpu.CompilerParams(vmem_limit_bytes=SMALL),
        cost_estimate=pl.CostEstimate(
            flops=20 * out.size, bytes_accessed=20 * out.size, transcendentals=out.size
        ),
        name="fresh_rows",
    )(*terms, *state)


def one_below(first, second, part=None):
    rows, width = first.shape[-2:]

    def kernel(first_ref, second_ref, out_ref):
        out_ref[:rows] = first_ref[...] if part is None else first_ref[part]
        out_ref[rows:] = second_ref[...] if part is None else second_ref[part]

    return pl.pallas_call(
        kernel,
        out_shape=jax.ShapeDtypeStruct((2 * rows, width), first.dtype),
        compiler_params=pltpu.CompilerParams(vmem_limit_bytes=SMALL),
        cost_estimate=pl.CostEstimate(
            flops=0, bytes_accessed=8 * rows * width, transcendentals=0
        ),
        name="one_below",
    )(first, second)


def staged(arrays):
    count = len(arrays)

    def kernel(*refs):
        for i in range(count):
            refs[count + i][...] = refs[i][...]

    rows, columns = arrays[0].shape
    return pl.pallas_call(
        kernel,
        grid=(2,),
        in_specs=[pl.BlockSpec((rows, columns // 2), lambda i: (0, i))] * count,
        out_specs=[pl.BlockSpec((rows, columns // 2), lambda i: (0, i))] * count,
        out_shape=[jax.ShapeDtypeStruct(x.shape, x.dtype) for x in arrays],
        compiler_params=pltpu.CompilerParams(vmem_limit_bytes=SMALL),
        cost_estimate=pl.CostEstimate(
            flops=0, bytes_accessed=8 * count * arrays[0].size, transcendentals=0
        ),
        name="staged",
    )(*arrays)


def packed_columns(hidden_rows, width, n_dp, n_replica):
    tokens = hidden_rows.shape[0]
    if width % HD:
        owner = lax.axis_index("dp") ^ jnp.arange(n_dp, dtype=jnp.int32)
        replica = lax.axis_index("replica") ^ jnp.arange(n_replica, dtype=jnp.int32)
        picks = owner[None, :] * n_replica + replica[:, None]
        cut = hidden_rows.reshape(tokens, -1, width)
        taken = jnp.take(cut, picks.reshape(-1), axis=1)
        taken = taken.reshape(tokens, n_replica, n_dp * width)
        return [taken[:, m] for m in range(n_replica)]

    def kernel(source_ref, *out_refs):
        dp, replica = lax.axis_index("dp"), lax.axis_index("replica")
        for m in range(n_replica):
            for o in range(n_dp):
                start = pl.multiple_of(((dp ^ o) * n_replica + (replica ^ m)) * width, width)
                out_refs[m][:, o * width : (o + 1) * width] = source_ref[:, pl.ds(start, width)]

    return pl.pallas_call(
        kernel,
        out_shape=[
            jax.ShapeDtypeStruct((tokens, n_dp * width), hidden_rows.dtype)
            for _ in range(n_replica)
        ],
        compiler_params=pltpu.CompilerParams(vmem_limit_bytes=16 * 2**20),
        cost_estimate=pl.CostEstimate(
            flops=0, bytes_accessed=4 * hidden_rows.size, transcendentals=0
        ),
        name="pack_hidden",
    )(hidden_rows)


def projected(token_blocks, pieces, width, before):
    count = len(token_blocks)
    parts = len(pieces)
    tokens = token_blocks[0].shape[0]
    widths = [piece.shape[1] for piece, _ in pieces]
    cuts = [slice(sum(widths[:i]), sum(widths[: i + 1])) for i in range(parts)]
    depth, columns = pieces[0][0].shape[0], sum(widths)

    def total_of(token_ref, weight_ref, places):
        total = None
        for i, place in enumerate(places):
            term = jnp.dot(
                token_ref[:, place * width : (place + 1) * width],
                weight_ref[i * width : (i + 1) * width, :],
                preferred_element_type=jnp.float32,
            )
            total = term if total is None else total + term
        return total

    def first_kernel(*refs):
        for m in range(count):
            for part in range(parts):
                total = total_of(refs[m], refs[count + part], pieces[part][1])
                refs[-1][m, :, cuts[part]] = total

    def last_kernel(*refs):
        kept_ref, away_ref = refs[-2], refs[-1]
        for m in range(count):
            for part in range(parts):
                cut = cuts[part]
                total = total_of(refs[m], refs[count + 1 + part], pieces[part][1])
                total = refs[count][m, :, cut] + total
                if m % 2:
                    away_ref[m // 2, :, cut] = total.astype(jnp.bfloat16)
                else:
                    kept_ref[m // 2, :, cut] = total

    cost = pl.CostEstimate(
        flops=2 * count * tokens * depth * columns,
        bytes_accessed=2 * count * tokens * depth * parts,
        transcendentals=0,
    )
    params = pltpu.CompilerParams(vmem_limit_bytes=24 * 2**20)
    weights = [piece for piece, _ in pieces]
    if before is None:
        return pl.pallas_call(
            first_kernel,
            out_shape=jax.ShapeDtypeStruct((count, tokens, columns), jnp.float32),
            compiler_params=params,
            cost_estimate=cost,
            name="projected_first",
        )(*token_blocks, *weights)
    return pl.pallas_call(
        last_kernel,
        out_shape=(
            jax.ShapeDtypeStruct((count // 2, tokens, columns), jnp.float32),
            jax.ShapeDtypeStruct((count // 2, tokens, columns), jnp.bfloat16),
        ),
        compiler_params=params,
        cost_estimate=cost,
        name="projected_last",
    )(*token_blocks, before, *weights)


def keys_and_numbers(keys_in, segment_ids):
    _, tokens, columns = keys_in.shape

    def kernel(key_ref, seg_ref, out_ref):
        out_ref[:tokens, :] = key_ref[0]
        numbers = seg_ref[...].astype(jnp.float32)
        numbers = jnp.concatenate([numbers] * (columns // tokens), axis=1)
        out_ref[tokens:, :] = jnp.broadcast_to(numbers, (16, columns)).astype(jnp.bfloat16)

    return pl.pallas_call(
        kernel,
        out_shape=jax.ShapeDtypeStruct((tokens + 16, columns), keys_in.dtype),
        compiler_params=pltpu.CompilerParams(vmem_limit_bytes=SMALL),
        name="keys_and_numbers",
    )(keys_in, segment_ids)


def attention_weights(packed_len, queries, key_blocks):
    tokens = queries.shape[1]
    heads_kv = key_blocks[0].shape[1] // HD
    groups = queries.shape[2] // (heads_kv * HD)
    spans = len(key_blocks)
    padded = key_blocks[0].shape[0]
    keys_all = spans * tokens

    def kernel(used_ref, q_ref, *rest):
        key_refs, out_ref = rest[:-1], rest[-1]
        here, used = lax.axis_index("dp"), used_ref[0]
        keys = jnp.concatenate(in_order(*[ref[0:tokens, :] for ref in key_refs]), axis=0)
        numbers = [ref[tokens : tokens + 16, :].astype(jnp.float32)[0:1, :] for ref in key_refs]
        seg_keys = jnp.concatenate(in_order(*numbers), axis=1)
        row = lax.broadcasted_iota(jnp.int32, (tokens, keys_all), 0)
        offset = lax.broadcasted_iota(jnp.int32, (tokens, keys_all), 1) - (spans - 1) * tokens
        seg_own = jnp.sum(jnp.where(offset == row, seg_keys, 0.0), axis=1, keepdims=True)
        allowed = (seg_own == seg_keys) & (offset <= row) & (offset + here * tokens >= 0)
        live = (here * tokens + lax.broadcasted_iota(jnp.int32, (tokens, 1), 0)) < used
        for j in range(groups):
            scores = lax.dot_general(
                q_ref[0, :, j * HD : (j + 1) * HD],
                keys,
                (((1,), (1,)), ((), ())),
                preferred_element_type=jnp.float32,
            ) * HD ** (-0.5)
            scores = jnp.where(allowed, scores, -1e30)
            weights = jnp.exp(scores - jnp.max(scores, axis=-1, keepdims=True))
            totals = jnp.sum(weights, axis=-1, keepdims=True)
            scale = jnp.where(live, 1.0 / totals, 0.0)
            out_ref[0, j * tokens : (j + 1) * tokens, :] = (weights * scale).astype(jnp.bfloat16)

    key_spec = pl.BlockSpec((padded, HD), lambda g: (0, g))
    return pl.pallas_call(
        kernel,
        grid=(heads_kv,),
        out_shape=jax.ShapeDtypeStruct((heads_kv, groups * tokens, keys_all), jnp.bfloat16),
        in_specs=[
            pl.BlockSpec(memory_space=pltpu.SMEM),
            pl.BlockSpec((1, tokens, groups * HD), lambda g: (0, 0, g)),
        ]
        + [key_spec] * spans,
        out_specs=pl.BlockSpec((1, groups * tokens, keys_all), lambda g: (g, 0, 0)),
        compiler_params=pltpu.CompilerParams(vmem_limit_bytes=16 * 2**20),
        cost_estimate=pl.CostEstimate(
            flops=2 * heads_kv * groups * tokens * keys_all * HD,
            bytes_accessed=2 * heads_kv * groups * tokens * (keys_all + HD),
            transcendentals=heads_kv * groups * tokens * keys_all,
        ),
        name="attention_weights",
    )(packed_len, queries, *key_blocks)


def weighted_values_early(weights, two_before, own):
    heads_kv, rows, _ = weights.shape
    tokens = own.shape[0]

    def kernel(w_ref, before_ref, own_ref, out_ref):
        for g in range(heads_kv):
            cut = slice(g * HD, (g + 1) * HD)
            picked = jnp.concatenate(
                [w_ref[g, :, tokens : 2 * tokens], w_ref[g, :, 3 * tokens : 4 * tokens]], axis=1
            )
            values = jnp.concatenate([before_ref[:, cut], own_ref[:, cut]], axis=0)
            out_ref[g] = jnp.dot(picked, values, preferred_element_type=jnp.float32)

    return pl.pallas_call(
        kernel,
        out_shape=jax.ShapeDtypeStruct((heads_kv, rows, HD), jnp.float32),
        compiler_params=pltpu.CompilerParams(vmem_limit_bytes=16 * 2**20),
        cost_estimate=pl.CostEstimate(
            flops=4 * heads_kv * rows * tokens * HD,
            bytes_accessed=4 * heads_kv * rows * tokens,
            transcendentals=0,
        ),
        name="weighted_values_early",
    )(weights, two_before, own)


def weighted_values(weights, early, leapt, relayed):
    heads_kv, rows, _ = weights.shape
    tokens = leapt.shape[0]
    groups = rows // tokens
    span = groups * HD

    def kernel(w_ref, early_ref, leapt_ref, relayed_ref, out_ref, mixed_ref, sems):
        copies = []
        for g in range(heads_kv):
            cut = slice(g * HD, (g + 1) * HD)
            picked = jnp.concatenate(
                [w_ref[g, :, 0:tokens], w_ref[g, :, 2 * tokens : 3 * tokens]], axis=1
            )
            oldest, _, last, _ = in_order(None, leapt_ref[:, cut], relayed_ref[:, cut], None)
            values = jnp.concatenate([oldest, last], axis=0)
            mixed = early_ref[g] + jnp.dot(picked, values, preferred_element_type=jnp.float32)
            for j in range(groups):
                mixed_ref[:, g * span + j * HD : g * span + (j + 1) * HD] = mixed[
                    j * tokens : (j + 1) * tokens, :
                ].astype(jnp.bfloat16)
            here = pl.ds(g * span, span)
            copies.append(
                pltpu.make_async_copy(mixed_ref.at[:, here], out_ref.at[0, :, here], sems.at[g])
            )
            copies[-1].start()
        for copy in copies:
            copy.wait()

    return pl.pallas_call(
        kernel,
        out_shape=jax.ShapeDtypeStruct((1, tokens, heads_kv * span), jnp.bfloat16),
        in_specs=[pl.BlockSpec(memory_space=pltpu.VMEM)] * 4,
        out_specs=pl.BlockSpec(memory_space=pltpu.HBM),
        scratch_shapes=[
            pltpu.VMEM((tokens, heads_kv * span), jnp.bfloat16),
            pltpu.SemaphoreType.DMA((heads_kv,)),
        ],
        compiler_params=pltpu.CompilerParams(vmem_limit_bytes=24 * 2**20),
        cost_estimate=pl.CostEstimate(
            flops=4 * heads_kv * rows * tokens * HD,
            bytes_accessed=4 * heads_kv * rows * tokens,
            transcendentals=0,
        ),
        name="weighted_values",
    )(weights, early, leapt, relayed)


def on_device(
    grad_parts,
    master_weight,
    moment_one,
    moment_two,
    queries,
    keys_in,
    hidden,
    segment_ids,
    packed_len,
):
    n_dp, n_replica = lax.axis_size("dp"), lax.axis_size("replica")
    tokens = queries.shape[1]
    rows, columns = master_weight.shape
    bits = bits_of(n_dp)
    orders = [bits, [bits[1], bits[0]] + bits[2:]]
    cuts = [(0, columns // 2), (columns // 2, columns // 2)]
    parts = len(orders)
    state = (master_weight, moment_one, moment_two)

    flips = [halving(order) for order in orders]
    away = blocks_taken(grad_parts, [part[: n_dp // 2] for part in flips], cuts)
    came = [swapped(block, order[0] * n_replica) for block, order in zip(away, orders)]
    kept = list(blocks_taken(grad_parts, [part[n_dp // 2 :] for part in flips], cuts))

    packed = packed_columns(hidden[0], rows, n_dp, n_replica)

    key_own = keys_and_numbers(keys_in, segment_ids)

    came[0], came[1], key_own = tied(came[0], came[1], key_own)
    key_blocks = preceding(key_own, False) + [key_own]
    streams = [[kept[part], came[part]] for part in range(parts)]
    token_blocks = [packed[0]] + [swapped(packed[m], m) for m in range(1, n_replica)]
    state_here = staged(state)

    left = n_dp // 2
    for step in range(1, len(bits)):
        for part in range(parts):
            mark = orders[part][step] * n_replica
            came[part] = swapped(first_half_sums([streams[part]], left)[0], mark)
        left = left // 2
        if step == 2:
            came[0], token_blocks[2] = tied(came[0], token_blocks[2])
        for part in range(parts):
            streams[part].append(came[part])

    fresh = [fresh_rows(terms, cut[0], state_here) for cut, terms in zip(cuts, streams)]
    grad_total = [
        sum(term[-1].astype(jnp.float32) for term in streams[part]) for part in range(parts)
    ]
    new_master, new_first, new_second = adam_update(jnp.concatenate(grad_total, axis=1), *state)
    labels = [[0] for _ in orders]
    for step in range(len(bits)):
        marks = [order[-1 - step] for order in orders]
        came = [swapped(fresh[part], marks[part] * n_replica) for part in range(parts)]
        if step == 0:
            came[0], token_blocks[1] = tied(came[0], token_blocks[1])
        if step == 1:
            came[0], token_blocks[3], key_blocks[1], key_blocks[2] = tied(
                came[0], token_blocks[3], key_blocks[1], key_blocks[2]
            )
            came[1], key_blocks[0] = tied(came[1], key_blocks[0])
        if step < len(bits) - 1:
            fresh = [one_below(fresh[part], came[part]) for part in range(parts)]
            labels = [own + [label ^ mark for label in own] for own, mark in zip(labels, marks)]
    weights = attention_weights(packed_len, queries, key_blocks)
    joined = fresh
    last = [[label ^ mark for label in own] for own, mark in zip(labels, marks)]
    before = projected(token_blocks, list(zip(joined, labels)), rows, None)
    *came, weights, before = tied(*came, weights, before)
    partial, leaving = projected(token_blocks, list(zip(came, last)), rows, before)

    came = swapped(leaving, 1)
    partial = partial + came.astype(jnp.float32)
    for bit in bits_of(n_replica)[1:]:
        partial = partial.reshape(-1, 2, tokens, columns)
        leaving = partial[:, 1].astype(jnp.bfloat16)
        came = swapped(leaving, bit)
        partial = partial[:, 0] + came.astype(jnp.float32)
    value = partial[0].astype(jnp.bfloat16)
    two_before, leapt, relayed = preceding(value, True)
    early = weighted_values_early(weights, two_before, value)
    attended = weighted_values(weights, early, leapt, relayed)
    return (new_master, new_first, new_second, attended)


def solution(mesh):
    in_specs = (
        P("dp", "replica", None),
        P(("dp", "replica"), None),
        P(("dp", "replica"), None),
        P(("dp", "replica"), None),
        P("replica", "dp", None),
        P("replica", "dp", None),
        P("replica", "dp", None),
        P("replica", "dp"),
        P("replica"),
    )
    out_specs = (
        P(("dp", "replica"), None),
        P(("dp", "replica"), None),
        P(("dp", "replica"), None),
        P("replica", "dp", None),
    )
    return jax.shard_map(
        on_device, mesh=mesh, in_specs=in_specs, out_specs=out_specs, check_vma=False
    )
```

```python
import jax
import jax.numpy as jnp
from jax import lax
from jax.experimental import pallas as pl
from jax.experimental.pallas import tpu as pltpu
from jax.sharding import PartitionSpec as P

HD = 128
ALL = ("dp", "replica")
SMALL = 12 * 2**20

beta_one = 0.9
beta_two = 0.95
bias_one = 1.0 - 0.9**10
bias_two = 1.0 - 0.95**10
adam_eps = 1e-08
learn_rate = 0.002
weight_decay = 0.1


def bits_of(count):
    return [1 << j for j in range(count.bit_length() - 1)]


def swapped(block, mask):
    total = lax.axis_size("dp") * lax.axis_size("replica")
    return lax.ppermute(block, ALL, [(i, i ^ mask) for i in range(total)])


def preceding(block, wraps):
    n_dp = lax.axis_size("dp")
    reach = n_dp if wraps else n_dp - 2
    two_before = lax.ppermute(block, "dp", [(i, (i + 2) % n_dp) for i in range(reach)])
    leaps = [(i, i + 1 + 2 * (i % 2)) for i in range(n_dp)]
    leapt = lax.ppermute(block, "dp", [leap for leap in leaps if leap[1] < n_dp])
    return [two_before, leapt, swapped(two_before, lax.axis_size("replica"))]


def in_order(two_before, leapt, relayed, own):
    odd = lax.axis_index("dp") % 2 == 1
    return [jnp.where(odd, relayed, leapt), two_before, jnp.where(odd, leapt, relayed), own]


def adam_update(grad_sum, master, moment_first, moment_second):
    first_new = beta_one * moment_first + (1.0 - beta_one) * grad_sum
    second_new = beta_two * moment_second + (1.0 - beta_two) * grad_sum * grad_sum
    step_dir = (
        first_new / bias_one / (jnp.sqrt(second_new / bias_two) + adam_eps) + weight_decay * master
    )
    master_new = master - learn_rate * step_dir
    return (master_new, first_new, second_new)


def tied(*values):
    return lax.optimization_barrier(values)


def halving(bits):
    if not bits:
        return [0]
    rest = halving(bits[1:])
    return [offset | bits[0] for offset in rest] + rest


def blocks_taken(terms, flips, cuts):
    _, rows, columns = terms.shape
    parts, blocks = len(flips), len(flips[0])

    def kernel(terms_ref, *refs):
        out_refs, sems = refs[:parts], refs[parts]
        here = lax.axis_index("dp")
        copies = []
        for part in range(parts):
            for i, flip in enumerate(flips[part]):
                copies.append(
                    pltpu.make_async_copy(
                        terms_ref.at[here ^ flip, :, pl.ds(*cuts[part])],
                        out_refs[part].at[i],
                        sems.at[part, i],
                    )
                )
        for copy in copies:
            copy.start()
        for copy in copies:
            copy.wait()

    return pl.pallas_call(
        kernel,
        in_specs=[pl.BlockSpec(memory_space=pltpu.HBM)],
        out_specs=[pl.BlockSpec(memory_space=pltpu.VMEM)] * parts,
        out_shape=[
            jax.ShapeDtypeStruct((blocks, rows, width), terms.dtype) for _, width in cuts
        ],
        scratch_shapes=[pltpu.SemaphoreType.DMA((parts, blocks))],
        compiler_params=pltpu.CompilerParams(vmem_limit_bytes=SMALL),
        cost_estimate=pl.CostEstimate(
            flops=0, bytes_accessed=4 * blocks * rows * columns, transcendentals=0
        ),
        name="blocks_taken",
    )(terms)


def first_half_sums(streams, left):
    count = len(streams)
    sizes = [len(terms) for terms in streams]
    _, rows, width = streams[0][0].shape

    def kernel(*refs):
        out_ref = refs[-1]
        at = 0
        for i, size in enumerate(sizes):
            for j in range(left // 2):
                total = None
                for ref in refs[at : at + size]:
                    term = ref[ref.shape[0] - left + j].astype(jnp.float32)
                    total = term if total is None else total + term
                out_ref[i, j] = total.astype(jnp.bfloat16)
            at += size

    out = jax.ShapeDtypeStruct((count, left // 2, rows, width), jnp.bfloat16)
    return pl.pallas_call(
        kernel,
        out_shape=out,
        compiler_params=pltpu.CompilerParams(vmem_limit_bytes=SMALL),
        cost_estimate=pl.CostEstimate(
            flops=2 * sizes[0] * out.size, bytes_accessed=8 * out.size, transcendentals=0
        ),
        name="first_half_sums",
    )(*[term for terms in streams for term in terms])


def fresh_rows(terms, start, state):
    _, rows, width = terms[0].shape

    def kernel(*refs):
        master_ref, first_ref, second_ref, out_ref = refs[-4:]
        grad = None
        for ref in refs[:-4]:
            term = ref[ref.shape[0] - 1].astype(jnp.float32)
            grad = term if grad is None else grad + term
        cut = slice(start, start + width)
        updated = adam_update(grad, master_ref[:, cut], first_ref[:, cut], second_ref[:, cut])
        out_ref[...] = updated[0].astype(jnp.bfloat16)

    out = jax.ShapeDtypeStruct((rows, width), jnp.bfloat16)
    return pl.pallas_call(
        kernel,
        out_shape=out,
        compiler_params=pltpu.CompilerParams(vmem_limit_bytes=SMALL),
        cost_estimate=pl.CostEstimate(
            flops=20 * out.size, bytes_accessed=20 * out.size, transcendentals=out.size
        ),
        name="fresh_rows",
    )(*terms, *state)


def one_below(first, second, part=None):
    rows, width = first.shape[-2:]

    def kernel(first_ref, second_ref, out_ref):
        out_ref[:rows] = first_ref[...] if part is None else first_ref[part]
        out_ref[rows:] = second_ref[...] if part is None else second_ref[part]

    return pl.pallas_call(
        kernel,
        out_shape=jax.ShapeDtypeStruct((2 * rows, width), first.dtype),
        compiler_params=pltpu.CompilerParams(vmem_limit_bytes=SMALL),
        cost_estimate=pl.CostEstimate(
            flops=0, bytes_accessed=8 * rows * width, transcendentals=0
        ),
        name="one_below",
    )(first, second)


def staged(arrays):
    count = len(arrays)

    def kernel(*refs):
        for i in range(count):
            refs[count + i][...] = refs[i][...]

    rows, columns = arrays[0].shape
    return pl.pallas_call(
        kernel,
        grid=(2,),
        in_specs=[pl.BlockSpec((rows, columns // 2), lambda i: (0, i))] * count,
        out_specs=[pl.BlockSpec((rows, columns // 2), lambda i: (0, i))] * count,
        out_shape=[jax.ShapeDtypeStruct(x.shape, x.dtype) for x in arrays],
        compiler_params=pltpu.CompilerParams(vmem_limit_bytes=SMALL),
        cost_estimate=pl.CostEstimate(
            flops=0, bytes_accessed=8 * count * arrays[0].size, transcendentals=0
        ),
        name="staged",
    )(*arrays)


def packed_columns(hidden_rows, width, n_dp, n_replica):
    tokens = hidden_rows.shape[0]
    if width % HD:
        owner = lax.axis_index("dp") ^ jnp.arange(n_dp, dtype=jnp.int32)
        replica = lax.axis_index("replica") ^ jnp.arange(n_replica, dtype=jnp.int32)
        picks = owner[None, :] * n_replica + replica[:, None]
        cut = hidden_rows.reshape(tokens, -1, width)
        taken = jnp.take(cut, picks.reshape(-1), axis=1)
        taken = taken.reshape(tokens, n_replica, n_dp * width)
        return [taken[:, m] for m in range(n_replica)]

    def kernel(source_ref, *out_refs):
        dp, replica = lax.axis_index("dp"), lax.axis_index("replica")
        for m in range(n_replica):
            for o in range(n_dp):
                start = pl.multiple_of(((dp ^ o) * n_replica + (replica ^ m)) * width, width)
                out_refs[m][:, o * width : (o + 1) * width] = source_ref[:, pl.ds(start, width)]

    return pl.pallas_call(
        kernel,
        out_shape=[
            jax.ShapeDtypeStruct((tokens, n_dp * width), hidden_rows.dtype)
            for _ in range(n_replica)
        ],
        compiler_params=pltpu.CompilerParams(vmem_limit_bytes=16 * 2**20),
        cost_estimate=pl.CostEstimate(
            flops=0, bytes_accessed=4 * hidden_rows.size, transcendentals=0
        ),
        name="pack_hidden",
    )(hidden_rows)


def projected(token_blocks, pieces, width, before):
    count = len(token_blocks)
    parts = len(pieces)
    tokens = token_blocks[0].shape[0]
    widths = [piece.shape[1] for piece, _ in pieces]
    cuts = [slice(sum(widths[:i]), sum(widths[: i + 1])) for i in range(parts)]
    depth, columns = pieces[0][0].shape[0], sum(widths)

    def total_of(token_ref, weight_ref, places):
        total = None
        for i, place in enumerate(places):
            term = jnp.dot(
                token_ref[:, place * width : (place + 1) * width],
                weight_ref[i * width : (i + 1) * width, :],
                preferred_element_type=jnp.float32,
            )
            total = term if total is None else total + term
        return total

    def first_kernel(*refs):
        for m in range(count):
            for part in range(parts):
                total = total_of(refs[m], refs[count + part], pieces[part][1])
                refs[-1][m, :, cuts[part]] = total

    def last_kernel(*refs):
        kept_ref, away_ref = refs[-2], refs[-1]
        for m in range(count):
            for part in range(parts):
                cut = cuts[part]
                total = total_of(refs[m], refs[count + 1 + part], pieces[part][1])
                total = refs[count][m, :, cut] + total
                if m % 2:
                    away_ref[m // 2, :, cut] = total.astype(jnp.bfloat16)
                else:
                    kept_ref[m // 2, :, cut] = total

    cost = pl.CostEstimate(
        flops=2 * count * tokens * depth * columns,
        bytes_accessed=2 * count * tokens * depth * parts,
        transcendentals=0,
    )
    params = pltpu.CompilerParams(vmem_limit_bytes=24 * 2**20)
    weights = [piece for piece, _ in pieces]
    if before is None:
        return pl.pallas_call(
            first_kernel,
            out_shape=jax.ShapeDtypeStruct((count, tokens, columns), jnp.float32),
            compiler_params=params,
            cost_estimate=cost,
            name="projected_first",
        )(*token_blocks, *weights)
    return pl.pallas_call(
        last_kernel,
        out_shape=(
            jax.ShapeDtypeStruct((count // 2, tokens, columns), jnp.float32),
            jax.ShapeDtypeStruct((count // 2, tokens, columns), jnp.bfloat16),
        ),
        compiler_params=params,
        cost_estimate=cost,
        name="projected_last",
    )(*token_blocks, before, *weights)


def keys_and_numbers(keys_in, segment_ids):
    _, tokens, columns = keys_in.shape

    def kernel(key_ref, seg_ref, out_ref):
        out_ref[:tokens, :] = key_ref[0]
        numbers = seg_ref[...].astype(jnp.float32)
        numbers = jnp.concatenate([numbers] * (columns // tokens), axis=1)
        out_ref[tokens:, :] = jnp.broadcast_to(numbers, (16, columns)).astype(jnp.bfloat16)

    return pl.pallas_call(
        kernel,
        out_shape=jax.ShapeDtypeStruct((tokens + 16, columns), keys_in.dtype),
        compiler_params=pltpu.CompilerParams(vmem_limit_bytes=SMALL),
        name="keys_and_numbers",
    )(keys_in, segment_ids)


def attention_weights(packed_len, queries, key_blocks):
    tokens = queries.shape[1]
    heads_kv = key_blocks[0].shape[1] // HD
    groups = queries.shape[2] // (heads_kv * HD)
    spans = len(key_blocks)
    padded = key_blocks[0].shape[0]
    keys_all = spans * tokens

    def kernel(used_ref, q_ref, *rest):
        key_refs, out_ref = rest[:-1], rest[-1]
        here, used = lax.axis_index("dp"), used_ref[0]
        keys = jnp.concatenate(in_order(*[ref[0:tokens, :] for ref in key_refs]), axis=0)
        numbers = [ref[tokens : tokens + 16, :].astype(jnp.float32)[0:1, :] for ref in key_refs]
        seg_keys = jnp.concatenate(in_order(*numbers), axis=1)
        row = lax.broadcasted_iota(jnp.int32, (tokens, keys_all), 0)
        offset = lax.broadcasted_iota(jnp.int32, (tokens, keys_all), 1) - (spans - 1) * tokens
        seg_own = jnp.sum(jnp.where(offset == row, seg_keys, 0.0), axis=1, keepdims=True)
        allowed = (seg_own == seg_keys) & (offset <= row) & (offset + here * tokens >= 0)
        live = (here * tokens + lax.broadcasted_iota(jnp.int32, (tokens, 1), 0)) < used
        for j in range(groups):
            scores = lax.dot_general(
                q_ref[0, :, j * HD : (j + 1) * HD],
                keys,
                (((1,), (1,)), ((), ())),
                preferred_element_type=jnp.float32,
            ) * HD ** (-0.5)
            scores = jnp.where(allowed, scores, -1e30)
            weights = jnp.exp(scores - jnp.max(scores, axis=-1, keepdims=True))
            totals = jnp.sum(weights, axis=-1, keepdims=True)
            scale = jnp.where(live, 1.0 / totals, 0.0)
            out_ref[0, j * tokens : (j + 1) * tokens, :] = (weights * scale).astype(jnp.bfloat16)

    key_spec = pl.BlockSpec((padded, HD), lambda g: (0, g))
    return pl.pallas_call(
        kernel,
        grid=(heads_kv,),
        out_shape=jax.ShapeDtypeStruct((heads_kv, groups * tokens, keys_all), jnp.bfloat16),
        in_specs=[
            pl.BlockSpec(memory_space=pltpu.SMEM),
            pl.BlockSpec((1, tokens, groups * HD), lambda g: (0, 0, g)),
        ]
        + [key_spec] * spans,
        out_specs=pl.BlockSpec((1, groups * tokens, keys_all), lambda g: (g, 0, 0)),
        compiler_params=pltpu.CompilerParams(vmem_limit_bytes=16 * 2**20),
        cost_estimate=pl.CostEstimate(
            flops=2 * heads_kv * groups * tokens * keys_all * HD,
            bytes_accessed=2 * heads_kv * groups * tokens * (keys_all + HD),
            transcendentals=heads_kv * groups * tokens * keys_all,
        ),
        name="attention_weights",
    )(packed_len, queries, *key_blocks)


def weighted_values_early(weights, two_before, leapt, own):
    heads_kv, rows, _ = weights.shape
    tokens = own.shape[0]

    def kernel(w_ref, before_ref, leapt_ref, own_ref, out_ref):
        leapt_at = pl.multiple_of(lax.axis_index("dp") % 2 * 2 * tokens, tokens)
        for g in range(heads_kv):
            cut = slice(g * HD, (g + 1) * HD)
            picked = jnp.concatenate(
                [
                    w_ref[g, :, tokens : 2 * tokens],
                    w_ref[g, :, 3 * tokens : 4 * tokens],
                    w_ref[g, :, pl.ds(leapt_at, tokens)],
                ],
                axis=1,
            )
            values = jnp.concatenate(
                [before_ref[:, cut], own_ref[:, cut], leapt_ref[:, cut]], axis=0
            )
            out_ref[g] = jnp.dot(picked, values, preferred_element_type=jnp.float32)

    return pl.pallas_call(
        kernel,
        out_shape=jax.ShapeDtypeStruct((heads_kv, rows, HD), jnp.float32),
        compiler_params=pltpu.CompilerParams(vmem_limit_bytes=16 * 2**20),
        cost_estimate=pl.CostEstimate(
            flops=4 * heads_kv * rows * tokens * HD,
            bytes_accessed=4 * heads_kv * rows * tokens,
            transcendentals=0,
        ),
        name="weighted_values_early",
    )(weights, two_before, leapt, own)


def weighted_values(weights, early, relayed):
    heads_kv, rows, _ = weights.shape
    tokens = relayed.shape[0]
    groups = rows // tokens
    span = groups * HD

    def kernel(w_ref, early_ref, relayed_ref, out_ref, mixed_ref, sems):
        relayed_at = pl.multiple_of((1 - lax.axis_index("dp") % 2) * 2 * tokens, tokens)
        copies = []
        for g in range(heads_kv):
            cut = slice(g * HD, (g + 1) * HD)
            mixed = early_ref[g] + jnp.dot(
                w_ref[g, :, pl.ds(relayed_at, tokens)],
                relayed_ref[:, cut],
                preferred_element_type=jnp.float32,
            )
            for j in range(groups):
                mixed_ref[:, g * span + j * HD : g * span + (j + 1) * HD] = mixed[
                    j * tokens : (j + 1) * tokens, :
                ].astype(jnp.bfloat16)
            here = pl.ds(g * span, span)
            copies.append(
                pltpu.make_async_copy(mixed_ref.at[:, here], out_ref.at[0, :, here], sems.at[g])
            )
            copies[-1].start()
        for copy in copies:
            copy.wait()

    return pl.pallas_call(
        kernel,
        out_shape=jax.ShapeDtypeStruct((1, tokens, heads_kv * span), jnp.bfloat16),
        in_specs=[pl.BlockSpec(memory_space=pltpu.VMEM)] * 3,
        out_specs=pl.BlockSpec(memory_space=pltpu.HBM),
        scratch_shapes=[
            pltpu.VMEM((tokens, heads_kv * span), jnp.bfloat16),
            pltpu.SemaphoreType.DMA((heads_kv,)),
        ],
        compiler_params=pltpu.CompilerParams(vmem_limit_bytes=24 * 2**20),
        cost_estimate=pl.CostEstimate(
            flops=4 * heads_kv * rows * tokens * HD,
            bytes_accessed=4 * heads_kv * rows * tokens,
            transcendentals=0,
        ),
        name="weighted_values",
    )(weights, early, relayed)


def on_device(
    grad_parts,
    master_weight,
    moment_one,
    moment_two,
    queries,
    keys_in,
    hidden,
    segment_ids,
    packed_len,
):
    n_dp, n_replica = lax.axis_size("dp"), lax.axis_size("replica")
    tokens = queries.shape[1]
    rows, columns = master_weight.shape
    bits = bits_of(n_dp)
    orders = [bits, [bits[1], bits[0]] + bits[2:]]
    cuts = [(0, columns // 2), (columns // 2, columns // 2)]
    parts = len(orders)
    state = (master_weight, moment_one, moment_two)

    flips = [halving(order) for order in orders]
    away = blocks_taken(grad_parts, [part[: n_dp // 2] for part in flips], cuts)
    came = [swapped(block, order[0] * n_replica) for block, order in zip(away, orders)]
    kept = list(blocks_taken(grad_parts, [part[n_dp // 2 :] for part in flips], cuts))

    packed = packed_columns(hidden[0], rows, n_dp, n_replica)

    key_own = keys_and_numbers(keys_in, segment_ids)

    came[0], came[1], key_own = tied(came[0], came[1], key_own)
    key_blocks = preceding(key_own, False) + [key_own]
    streams = [[kept[part], came[part]] for part in range(parts)]
    token_blocks = [packed[0]] + [swapped(packed[m], m) for m in range(1, n_replica)]
    state_here = staged(state)

    left = n_dp // 2
    for step in range(1, len(bits)):
        for part in range(parts):
            mark = orders[part][step] * n_replica
            came[part] = swapped(first_half_sums([streams[part]], left)[0], mark)
        left = left // 2
        if step == 2:
            came[0], token_blocks[2] = tied(came[0], token_blocks[2])
        for part in range(parts):
            streams[part].append(came[part])

    fresh = [fresh_rows(terms, cut[0], state_here) for cut, terms in zip(cuts, streams)]
    grad_total = [
        sum(term[-1].astype(jnp.float32) for term in streams[part]) for part in range(parts)
    ]
    new_master, new_first, new_second = adam_update(jnp.concatenate(grad_total, axis=1), *state)
    labels = [[0] for _ in orders]
    for step in range(len(bits)):
        marks = [order[-1 - step] for order in orders]
        came = [swapped(fresh[part], marks[part] * n_replica) for part in range(parts)]
        if step == 0:
            came[0], token_blocks[1] = tied(came[0], token_blocks[1])
        if step == 1:
            came[0], token_blocks[3], key_blocks[1], key_blocks[2] = tied(
                came[0], token_blocks[3], key_blocks[1], key_blocks[2]
            )
            came[1], key_blocks[0] = tied(came[1], key_blocks[0])
        if step < len(bits) - 1:
            fresh = [one_below(fresh[part], came[part]) for part in range(parts)]
            labels = [own + [label ^ mark for label in own] for own, mark in zip(labels, marks)]
    weights = attention_weights(packed_len, queries, key_blocks)
    joined = fresh
    last = [[label ^ mark for label in own] for own, mark in zip(labels, marks)]
    before = projected(token_blocks, list(zip(joined, labels)), rows, None)
    *came, weights, before = tied(*came, weights, before)
    partial, leaving = projected(token_blocks, list(zip(came, last)), rows, before)

    came = swapped(leaving, 1)
    partial = partial + came.astype(jnp.float32)
    for bit in bits_of(n_replica)[1:]:
        partial = partial.reshape(-1, 2, tokens, columns)
        leaving = partial[:, 1].astype(jnp.bfloat16)
        came = swapped(leaving, bit)
        partial = partial[:, 0] + came.astype(jnp.float32)
    value = partial[0].astype(jnp.bfloat16)
    two_before, leapt, relayed = preceding(value, True)
    early = weighted_values_early(weights, two_before, leapt, value)
    attended = weighted_values(weights, early, relayed)
    return (new_master, new_first, new_second, attended)


def solution(mesh):
    in_specs = (
        P("dp", "replica", None),
        P(("dp", "replica"), None),
        P(("dp", "replica"), None),
        P(("dp", "replica"), None),
        P("replica", "dp", None),
        P("replica", "dp", None),
        P("replica", "dp", None),
        P("replica", "dp"),
        P("replica"),
    )
    out_specs = (
        P(("dp", "replica"), None),
        P(("dp", "replica"), None),
        P(("dp", "replica"), None),
        P("replica", "dp", None),
    )
    return jax.shard_map(
        on_device, mesh=mesh, in_specs=in_specs, out_specs=out_specs, check_vma=False
    )
```
